128 devices in a mesh: section: 2 (over core), block: 64 (over x, z, y).
Axes of the slice: x: 4, y: 4, z: 4, core: 2. Of those that a mesh axis runs over, the one named last changes fastest.
Arguments:
- env: float32 [2, 256, 512, 512], P('section', 'block'), may hold values from -6 to 6
- site: float32 [2, 8192, 2, 512], P('section', 'block'), may hold values from -0.25 to 0.25
- sector_tiles: int32 [16], replicated, may hold values from 1 to 16, 128 in all
- mpo_mask: int32 [2, 16, 16], P('section'), may hold values 0 or 1
- mpo_coef: float32 [2, 2, 16, 16], P('section'), may hold values from -1.5 to 1.5
- psi: float32 [2, 8192, 512], P('section', 'block'), may hold values from -0.03125 to 0.03125
- center_coef: float32 [2, 16], P('section'), may hold values from -1.5 to 1.5
Outputs:
- new_env: float32 [2, 256, 512, 512], P('section', 'block')
- hpsi: float32 [2, 8192, 512], P('section', 'block')
The draws below stay inside these ranges and needn't reach their ends.
Inputs may be any that keep to these rules, and one draw needn't show every extreme that they name: Sector q holds 32 * sector_tiles[q] states; the entries sum to M // 32 and the largest equals 16.
All inputs are finite; a program needn't handle non-finite values. No bound on the sum of `mpo_mask` on one device may be relied on, other than what follows from the above.
Results may differ from the reference program's by a relative error of at most 0.0003.
Values sent between devices are 32-bit elements; how exact they have to be, the bound alone decides.
A program may use at most 192 MiB of HBM per device.

```python
import math
import jax
import jax.numpy as jnp
import numpy as np
from jax import lax

M = 4096
NSEC = 16
TROW = 32
MOST = 16
W = 16
SMAX = 512


def touch_ends(values, stream_key, smallest, largest):
    longest = values.shape.index(max(values.shape))
    spots = []
    for shift in (0, 1):
        where = [jax.random.randint(jax.random.fold_in(stream_key, axis), (), 0, length) for axis, length in enumerate(values.shape)]
        where[longest] = (where[longest] + shift) % values.shape[longest]
        spots.append(tuple(where))
    return values.at[spots[0]].set(smallest).at[spots[1]].set(largest)


def level_of(key, extent, shards, least, high):
    gain, own = 1.0, jax.random.fold_in(key, 6)
    for position, blocks in shards:
        heights = jnp.exp(jax.random.uniform(jax.random.fold_in(own, position), (blocks,), jnp.float32, least / len(shards), high / len(shards)))
        gain = gain * jnp.repeat(heights, extent[position] // blocks).reshape([-1 if axis == position else 1 for axis in range(len(extent))])
    return gain


def profile(number_of, total, bound, lean):
    loads = [(1 << 20) // math.isqrt(standing ** lean) + 1 for standing in range(2, number_of + 1)]
    surplus, holding = total - bound - (number_of - 1), [1] * (number_of - 1)
    while surplus > 0:
        free = [i for i in range(number_of - 1) if holding[i] < bound]
        pool, budget = sum([loads[i] for i in free]), surplus
        for i in free:
            addition = min(bound - holding[i], max(1, budget * loads[i] // pool), surplus)
            holding[i] = holding[i] + addition
            surplus = surplus - addition
    return np.array([bound] + holding)


def uneven_parts(own_key, amount, total, limit, skew):
    if amount == 2:
        one = jax.random.randint(own_key, (), max(1, total - limit), min(limit, total - 1) + 1)
        return jnp.stack([one, total - one])
    lengths = jnp.asarray(profile(amount, total, limit, skew), jnp.int32)
    twos = (amount - 1) // 2
    giver, receiver = lengths[1:1 + 2 * twos:2], lengths[2:2 + 2 * twos:2]
    room = jnp.minimum(giver - 1, limit - receiver)
    shifted = jax.random.randint(jax.random.fold_in(own_key, 1), (twos,), 0, 1 << 20) % (room + 1)
    lengths = lengths.at[1:1 + 2 * twos:2].set(giver - shifted).at[2:2 + 2 * twos:2].set(receiver + shifted)
    return lengths[jax.random.permutation(jax.random.fold_in(own_key, 2), amount)]


def normal_values(key, dims, deviation, limit, cuts=(), kind=jnp.bfloat16):
    loudness = level_of(key, dims, cuts, -0.22, 0.18) if cuts else 1.0
    array = jax.random.normal(key, dims, jnp.float32) * deviation * loudness
    return jnp.minimum(jnp.maximum(array, -limit), limit).astype(kind)


def setup_inputs(seed: int = 0) -> dict:
    keys = jax.random.split(jax.random.key(seed), 8)
    env = normal_values(keys[0], (2, NSEC * W, SMAX, SMAX), 1.0, 6.0, ((0, 2), (1, 64)), jnp.float32)
    site = normal_values(keys[1], (2, NSEC * SMAX, 2, SMAX), SMAX ** -0.5, 0.25, ((0, 2), (1, 64)), jnp.float32)
    sector_tiles = uneven_parts(keys[2], NSEC, M // TROW, MOST, 2).astype(jnp.int32)
    mpo_mask = touch_ends((jax.random.randint(keys[3], (2, W, W), 0, 2) < 1).astype(jnp.int32), jax.random.fold_in(keys[3], 1), 0, 1)
    mpo_coef = normal_values(keys[4], (2, 2, W, W), W ** -0.5, 1.5, ((0, 2),), jnp.float32)
    psi = normal_values(keys[5], (2, NSEC * SMAX, SMAX), (SMAX * SMAX // 8) ** -0.5, 0.03125, ((0, 2), (1, 64)), jnp.float32)
    center_coef = normal_values(keys[6], (2, W), W ** -0.5, 1.5, ((0, 2),), jnp.float32)
    return {"env": env, "site": site, "sector_tiles": sector_tiles, "mpo_mask": mpo_mask, "mpo_coef": mpo_coef, "psi": psi, "center_coef": center_coef}


HIGH = lax.Precision.HIGHEST


def reference(env, site, sector_tiles, mpo_mask, mpo_coef, psi, center_coef):
    sizes = jnp.concatenate([sector_tiles * TROW, jnp.zeros((1,), jnp.int32)])
    span = jnp.arange(SMAX, dtype=jnp.int32)
    fresh_envs = []
    for section in range(2):
        env_here = env[section].reshape(NSEC, W, SMAX, SMAX)
        site_here = site[section].reshape(NSEC, SMAX, 2, SMAX)
        mixing = mpo_coef[section] * mpo_mask[section].astype(jnp.float32)

        def absorb(sector):
            blocks = env_here[sector]
            tensor = site_here[sector]
            row_keep = (span < sizes[sector]).astype(jnp.float32)
            results = []
            for spin in range(2):
                col_keep = (span < sizes[sector + spin]).astype(jnp.float32)
                masked = tensor[:, spin, :] * row_keep[:, None] * col_keep[None, :]
                inner = jnp.einsum("wij,jk->wik", blocks, masked, precision=HIGH)
                outer = jnp.einsum("ji,wjk->wik", masked, inner, precision=HIGH)
                results.append(jnp.einsum("wv,wij->vij", mixing[spin], outer, precision=HIGH))
            return results[0], results[1]

        stay_terms, rise_terms = lax.map(absorb, jnp.arange(NSEC, dtype=jnp.int32))
        carried = jnp.concatenate([jnp.zeros((1, W, SMAX, SMAX), jnp.float32), rise_terms[:-1]], axis=0)
        fresh_envs.append(stay_terms + carried)
    left_env, right_env = fresh_envs
    outputs = []
    for pair in range(2):
        wave = psi[pair].reshape(NSEC, SMAX, SMAX)

        def apply_block(sector):
            first = jnp.einsum("wij,jk->wik", left_env[sector], wave[sector], precision=HIGH)
            second = jnp.einsum("wij,wjk->wik", first, right_env[sector], precision=HIGH)
            return jnp.einsum("w,wik->ik", center_coef[pair], second, precision=HIGH)

        outputs.append(lax.map(apply_block, jnp.arange(NSEC, dtype=jnp.int32)).reshape(NSEC * SMAX, SMAX))
    new_env = jnp.stack([left_env.reshape(NSEC * W, SMAX, SMAX), right_env.reshape(NSEC * W, SMAX, SMAX)])
    return new_env, jnp.stack(outputs)
```

```python
import functools

import jax
import jax.numpy as jnp
from jax import lax
from jax.experimental import pallas as pl
from jax.experimental.pallas import tpu as pltpu
from jax.sharding import PartitionSpec as P

TROW = 32
CH = 32
NE = 16
NK = NE + 3
PSI = NK - 1
AHEAD = 3
MESH = pl.DeviceIdType.MESH
F32, BF16 = jnp.float32, jnp.bfloat16


def halves(value):
    high = value.astype(BF16)
    low = (value - high.astype(F32)).astype(BF16)
    return high, low


def dot3(ah, al, bh, bl):
    dot = functools.partial(jnp.dot, preferred_element_type=F32)
    return dot(ah, bh) + (dot(ah, bl) + dot(al, bh))


def kernel(nsector, env, site, psi, tiles, mask, coef, center, fresh, hpsi,
           own, rcv, f0, f1s, f1r, hbuf, z, zp, abuf, pbuf, q, s1, s2, table,
           load_sem, shift_sem, own_send, own_recv, fwd_send, fwd_recv,
           f1_send, f1_recv, zp_send, zp_recv, out_sem, rs_send, rs_recv):
    section = lax.axis_index("section")
    block = lax.axis_index("block")
    nblock = nsector * 4
    sector = block // 4
    y = block % 4
    base = block - y
    right = (section, base + (y + 1) % 4)
    left = (section, base + (y + 3) % 4)
    above = (section, (block + 4) % nblock)
    below = (section, (block + nblock - 4) % nblock)
    other = (1 - section, block)

    def remote(src, dst, send, recv, to):
        return pltpu.make_async_remote_copy(
            src_ref=src, dst_ref=dst, send_sem=send, recv_sem=recv, device_id=to, device_id_type=MESH)

    def load(k):
        if isinstance(k, int) and k == 0:
            src = site.at[0]
        elif isinstance(k, int) and k == PSI:
            src = psi
        else:
            src = env.at[:, pl.ds(pl.multiple_of((k - 2) * CH, CH), CH), :]
        return pltpu.make_async_copy(src, own.at[k], load_sem.at[k])

    load(0).start()
    lax.fori_loop(2, 2 + NE, lambda k, c: (load(k).start(), c)[1], 0)
    load(PSI).start()

    barrier = pltpu.get_barrier_semaphore()
    for peer in (right, left, above, below, other):
        pl.semaphore_signal(barrier, inc=1, device_id=peer, device_id_type=MESH)
    pl.semaphore_wait(barrier, 5)

    def shift():
        return remote(site.at[1], own.at[1], shift_sem.at[0], shift_sem.at[1], above)

    def to_right(k):
        return remote(own.at[k], rcv.at[2, k], own_send.at[0, k], own_recv.at[0, k], right)

    def to_left(k):
        return remote(own.at[k], rcv.at[0, k], own_send.at[1, k], own_recv.at[1, k], left)

    def on_right(k):
        return remote(rcv.at[2, k, pl.ds(0, 2)], rcv.at[1, k, pl.ds(0, 2)],
                      fwd_send.at[0, k], fwd_recv.at[0, k], right)

    def on_left(k):
        return remote(rcv.at[0, k, pl.ds(2, 2)], rcv.at[1, k, pl.ds(2, 2)],
                      fwd_send.at[1, k], fwd_recv.at[1, k], left)

    def issue(k):
        to_right(k).start()
        to_left(k).start()

    def relay(k):
        to_right(k).wait_recv()
        on_right(k).start()
        to_left(k).wait_recv()
        on_left(k).start()

    def arrived(k):
        on_right(k).wait_recv()
        on_left(k).wait_recv()

    shift().start()
    load(0).wait()
    issue(0)
    load(2).wait()
    issue(2)
    shift().wait_recv()
    issue(1)

    for s in range(2):
        for d in range(4):
            for j in range(4):
                w = ((y + d) % 4) * 4 + j
                for v in range(4):
                    c = coef[0, s, w, y * 4 + v] * mask[0, w, y * 4 + v].astype(F32)
                    table[(s * 4 + v) * 16 + d * 4 + j] = c

    size_here = tiles[sector] * TROW
    size_prev = jnp.where(sector > 0, tiles[jnp.maximum(sector - 1, 0)] * TROW, 0)

    def piece(d, k):
        return own[k] if d == 0 else rcv[d - 1, k]

    def assemble(s, k, rows_kept):
        for d in range(4):
            row0 = pl.multiple_of(((y + d) % 4) * 128, 128)
            v = piece(d, k).reshape(128, 512)
            i = lax.broadcasted_iota(jnp.int32, (128, 512), 0) + row0
            j = lax.broadcasted_iota(jnp.int32, (128, 512), 1)
            v = jnp.where((i < rows_kept) & (j < size_here), v, 0.0)
            t = v.T
            for h, (a, b) in enumerate(zip(halves(v), halves(t))):
                abuf[s * 2 + h, pl.ds(row0, 128), :] = a
                abuf[4 + s * 2 + h, :, pl.ds(row0, 128)] = b

    def f1(e):
        return remote(f1s.at[e], f1r.at[e], f1_send.at[e], f1_recv.at[e], above)

    def mix(e, i):
        k = e + 2

        def rows(r, c):
            span = pl.ds(pl.multiple_of(r * 8, 8), 8)
            acc = [None] * 8
            for d in range(4):
                for j in range(4):
                    x = own[k, j, span, :] if d == 0 else rcv[d - 1, k, j, span, :]
                    for o in range(8):
                        term = table[o * 16 + d * 4 + j] * x
                        acc[o] = term if acc[o] is None else acc[o] + term
            for v in range(4):
                f0[i, v, span, :] = acc[v]
                f1s[e, v, span, :] = acc[4 + v]
            return c

        lax.fori_loop(0, CH // 8, rows, 0)
        f1(e).start()

    def first(s, g):
        def half(t, c):
            lhs = f0[pl.ds(2 * t, 2)] if s == 0 else f1r[pl.ds(4 * g + 2 * t, 2)]
            ah, al = halves(lhs.reshape(256, 512))
            r = dot3(ah, al, abuf[s * 2], abuf[s * 2 + 1])
            for h, part in enumerate(halves(r)):
                part = part.reshape(2, 4, CH, 512)
                for u in range(2):
                    at = pl.multiple_of((g % 2) * 128 + (2 * t + u) * CH, CH)
                    for v in range(4):
                        hbuf[s, h, v, pl.ds(at, CH), :] = part[u, v]
            return c

        lax.fori_loop(0, 2, half, 0)

    def second(half, v):
        cols = pl.ds(half * 256, 256)
        r = None
        for s in range(2):
            t = dot3(abuf[4 + s * 2, :, cols], abuf[5 + s * 2, :, cols], hbuf[s, 0, v], hbuf[s, 1, v])
            r = t if r is None else r + t
        if half == 0:
            z[v] = r
        else:
            z[v] += r

    load(3).wait()
    issue(3)
    relay(0)
    load(4).wait()
    issue(4)
    relay(1)
    arrived(0)
    assemble(0, 0, size_here)
    load(5).wait()
    issue(5)
    relay(2)
    arrived(1)
    assemble(1, 1, size_prev)

    for g in range(4):
        def step(i, c, g=g):
            e = g * 4 + i
            k = e + 3

            @pl.when(e <= NE - 5)
            def _():
                load(k + AHEAD).wait()
                issue(k + AHEAD)

            if g == 3:
                @pl.when(e == NE - 4)
                def _():
                    load(PSI).wait()
                    issue(PSI)

            relay(k)
            arrived(k - 1)
            mix(e, i)
            return c

        lax.fori_loop(0, 4, step, 0)
        if g > 0:
            lax.fori_loop(4 * g - 4, 4 * g, lambda e, c: (f1(e).wait_recv(), c)[1], 0)
            first(1, g - 1)
        if g == 2:
            lax.fori_loop(0, 4, lambda v, c: (second(0, v), c)[1], 0)
        first(0, g)

    arrived(PSI)
    for d in range(4):
        row0 = pl.multiple_of(((y + d) % 4) * 128, 128)
        for h, part in enumerate(halves(piece(d, PSI).reshape(128, 512))):
            pbuf[h, pl.ds(row0, 128), :] = part

    lax.fori_loop(12, 16, lambda e, c: (f1(e).wait_recv(), c)[1], 0)
    first(1, 3)

    def exchange(v):
        return remote(z.at[v], zp.at[v], zp_send.at[v], zp_recv.at[v], other)

    def out(v):
        return pltpu.make_async_copy(z.at[v], fresh.at[v], out_sem.at[v])

    def finish(v, c):
        second(1, v)
        exchange(v).start()
        out(v).start()
        return c

    lax.fori_loop(0, 4, finish, 0)

    def apply_left(v, c):
        exchange(v).wait_recv()
        lh, ll = halves(jnp.where(section == 0, z[v], zp[v]))
        x = dot3(lh, ll, pbuf[0], pbuf[1]) * center[0, y * 4 + v]
        for h, part in enumerate(halves(x)):
            hbuf[0, h, v] = part[:256]
            hbuf[1, h, v] = part[256:]
        rh, rl = halves(jnp.where(section == 0, zp[v], z[v]))
        abuf[2 * v] = rh
        abuf[2 * v + 1] = rl
        return c

    lax.fori_loop(0, 4, apply_left, 0)

    def partial(b):
        rows = pl.ds(pl.multiple_of((b % 2) * 128, 128), 128)
        r = None
        for v in range(4):
            t = dot3(hbuf[b // 2, 0, v, rows, :], hbuf[b // 2, 1, v, rows, :], abuf[2 * v], abuf[2 * v + 1])
            r = t if r is None else r + t
        return r

    hops = [
        remote(q.at[0, 0], s1.at[0], rs_send.at[0], rs_recv.at[0], right),
        remote(q.at[0, 1], s1.at[1], rs_send.at[1], rs_recv.at[1], left),
        remote(q.at[1], s2.at[0], rs_send.at[2], rs_recv.at[2], right),
        remote(q.at[2], s2.at[1], rs_send.at[3], rs_recv.at[3], left),
    ]

    def keep(slot, r):
        q[slot, 0] = r[:, :256]
        q[slot, 1] = r[:, 256:]

    keep(0, partial((y + 2) % 4))
    hops[0].start()
    hops[1].start()
    keep(1, partial((y + 1) % 4))
    hops[0].wait_recv()
    q[1, 0] += s1[0]
    hops[2].start()
    keep(2, partial((y + 3) % 4))
    hops[1].wait_recv()
    q[2, 1] += s1[1]
    hops[3].start()
    keep(3, partial(y))
    hops[2].wait_recv()
    hops[3].wait_recv()
    for t in range(2):
        hpsi[:, pl.ds(t * 256, 256)] = q[3, t] + (s2[0, t] + s2[1, t])

    for hop in hops:
        hop.wait_send()
    shift().wait_send()

    def drain(k, c):
        to_right(k).wait_send()
        to_left(k).wait_send()
        on_right(k).wait_send()
        on_left(k).wait_send()
        return c

    lax.fori_loop(0, NK, drain, 0)
    lax.fori_loop(0, NE, lambda e, c: (f1(e).wait_send(), c)[1], 0)

    def last(v, c):
        exchange(v).wait_send()
        out(v).wait()
        return c

    lax.fori_loop(0, 4, last, 0)


def local(env, site, sector_tiles, mpo_mask, mpo_coef, psi, center_coef):
    spins = site[0].transpose(1, 0, 2).reshape(2, 4, CH, 512)
    anywhere = pl.BlockSpec(memory_space=pl.ANY)
    scalars = pl.BlockSpec(memory_space=pltpu.SMEM)
    dma = pltpu.SemaphoreType.DMA
    fresh, hpsi = pl.pallas_call(
        functools.partial(kernel, sector_tiles.shape[0]),
        out_shape=(
            jax.ShapeDtypeStruct((4, 512, 512), F32),
            jax.ShapeDtypeStruct((128, 512), F32),
        ),
        in_specs=[anywhere, anywhere, anywhere, scalars, scalars, scalars, scalars],
        out_specs=(anywhere, pl.BlockSpec(memory_space=pltpu.VMEM)),
        scratch_shapes=[
            pltpu.VMEM((NK, 4, CH, 512), F32),
            pltpu.VMEM((3, NK, 4, CH, 512), F32),
            pltpu.VMEM((4, 4, CH, 512), F32),
            pltpu.VMEM((NE, 4, CH, 512), F32),
            pltpu.VMEM((NE, 4, CH, 512), F32),
            pltpu.VMEM((2, 2, 4, 256, 512), BF16),
            pltpu.VMEM((4, 512, 512), F32),
            pltpu.VMEM((4, 512, 512), F32),
            pltpu.VMEM((8, 512, 512), BF16),
            pltpu.VMEM((2, 512, 512), BF16),
            pltpu.VMEM((4, 2, 128, 256), F32),
            pltpu.VMEM((2, 128, 256), F32),
            pltpu.VMEM((2, 2, 128, 256), F32),
            pltpu.SMEM((128,), F32),
            dma((NK,)), dma((2,)), dma((2, NK)), dma((2, NK)), dma((2, NK)), dma((2, NK)),
            dma((NE,)), dma((NE,)), dma((4,)), dma((4,)), dma((4,)), dma((4,)), dma((4,)),
        ],
        compiler_params=pltpu.CompilerParams(
            collective_id=0, has_side_effects=True, vmem_limit_bytes=60 << 20
        ),
        name="window",
    )(env[0], spins, psi[0].reshape(4, CH, 512), sector_tiles, mpo_mask, mpo_coef, center_coef)
    return fresh[None], hpsi[None]


def solution(mesh):
    placed = (
        P("section", "block", None, None),
        P("section", "block", None, None),
        P(),
        P("section", None, None),
        P("section", None, None, None),
        P("section", "block", None),
        P("section", None),
    )
    return jax.shard_map(
        local,
        mesh=mesh,
        in_specs=placed,
        out_specs=(P("section", "block", None, None), P("section", "block", None)),
        check_vma=False,
    )
```

```python
import functools

import jax
import jax.numpy as jnp
from jax import lax
from jax.experimental import pallas as pl
from jax.experimental.pallas import tpu as pltpu
from jax.sharding import PartitionSpec as P

TROW = 32
CH = 32
UR = 16
NL = 8
LOW = (0, 1, 2, 9, 10, 11, 12, 13)
A0, A1, PSI = 3, 8, 14
SHARED = (4, 5, 6, 7)
NK = 15
MESH = pl.DeviceIdType.MESH
F32, BF16 = jnp.float32, jnp.bfloat16


def halves(value):
    high = value.astype(BF16)
    low = (value - high.astype(F32)).astype(BF16)
    return high, low


def dot3(ah, al, bh, bl):
    dot = functools.partial(jnp.dot, preferred_element_type=F32)
    return dot(ah, bh) + (dot(ah, bl) + dot(al, bh))


def kernel(nsector, env, site, psi, tiles, mask, coef, center, fresh, hpsi,
           own, rcv, f0, f1s, f1r, up, pack, got, fu, back0, back1, hbuf, z, zp, abuf, pbuf, q, s1, s2, table, place,
           load_sem, up_sem, shift_sem, own_send, own_recv, fwd_send, fwd_recv, f1_send, f1_recv,
           sh_send, sh_recv, bk_send, bk_recv, zp_send, zp_recv, out_sem, rs_send, rs_recv):
    section = lax.axis_index("section")
    block = lax.axis_index("block")
    sector = block // 4
    y = block % 4
    base = block - y
    right = (section, base + (y + 1) % 4)
    left = (section, base + (y + 3) % 4)
    other = (1 - section, block)

    def ring(distance):
        return (section, ((sector + distance + nsector) % nsector) * 4 + y)

    above = ring(1)

    def remote(src, dst, send, recv, to):
        return pltpu.make_async_remote_copy(
            src_ref=src, dst_ref=dst, send_sem=send, recv_sem=recv, device_id=to, device_id_type=MESH)

    def loop(lo, hi, body):
        lax.fori_loop(lo, hi, lambda i, c: (body(i), c)[1], 0)

    def load(k):
        if k == A0:
            src = site.at[0]
        elif k == PSI:
            src = psi
        else:
            src = env.at[:, pl.ds(LOW.index(k) * CH, CH), :]
        return pltpu.make_async_copy(src, own.at[k], load_sem.at[k])

    def load_up(u):
        rows = pl.ds(pl.multiple_of(256 + u * UR, UR), UR)
        return pltpu.make_async_copy(env.at[:, rows, :], up.at[u], up_sem.at[u])

    load(0).start()
    loop(0, nsector, lambda u: load_up(u).start())
    for k in LOW[1:] + (A0, PSI):
        load(k).start()

    barrier = pltpu.get_barrier_semaphore()
    for peer in (right, left, other):
        pl.semaphore_signal(barrier, inc=1, device_id=peer, device_id_type=MESH)
    loop(1, nsector, lambda d: pl.semaphore_signal(barrier, inc=1, device_id=ring(d), device_id_type=MESH))
    pl.semaphore_wait(barrier, nsector + 2)

    def shift():
        return remote(site.at[1], own.at[A1], shift_sem.at[0], shift_sem.at[1], above)

    def rows_of(k):
        return pl.ds(0, UR if k == SHARED[3] else CH)

    def to_right(k):
        r = rows_of(k)
        return remote(own.at[k, :, r], rcv.at[2, k, :, r], own_send.at[0, k], own_recv.at[0, k], right)

    def to_left(k):
        r = rows_of(k)
        return remote(own.at[k, :, r], rcv.at[0, k, :, r], own_send.at[1, k], own_recv.at[1, k], left)

    def on_right(k):
        r = rows_of(k)
        return remote(rcv.at[2, k, pl.ds(0, 2), r], rcv.at[1, k, pl.ds(0, 2), r],
                      fwd_send.at[0, k], fwd_recv.at[0, k], right)

    def on_left(k):
        r = rows_of(k)
        return remote(rcv.at[0, k, pl.ds(2, 2), r], rcv.at[1, k, pl.ds(2, 2), r],
                      fwd_send.at[1, k], fwd_recv.at[1, k], left)

    def issue(k):
        if k in LOW + (A0, PSI):
            load(k).wait()
        to_right(k).start()
        to_left(k).start()

    def relay(k):
        to_right(k).wait_recv()
        on_right(k).start()
        to_left(k).wait_recv()
        on_left(k).start()

    def arrived(k):
        on_right(k).wait_recv()
        on_left(k).wait_recv()

    issue(0)

    start = 0
    for i in range(nsector):
        count = jnp.maximum(2 * (tiles[i] - 8), 0)
        place[i] = start % 16
        place[16 + i] = count
        start = start + count

    def share(d):
        return remote(pack.at[d], got.at[d], sh_send.at[d], sh_recv.at[d], ring(d))

    loop(0, nsector, lambda u: load_up(u).wait())

    def unit_for(d):
        return (sector + d + 16 - place[sector]) % 16

    got[0] = up[unit_for(0)]

    def send_share(d):
        pack[d] = up[unit_for(d)]
        share(d).start()

    loop(1, nsector, send_share)
    shift().start()
    issue(1)
    issue(2)

    for s in range(2):
        for d in range(4):
            for j in range(4):
                w = ((y + d) % 4) * 4 + j
                for v in range(4):
                    c = coef[0, s, w, y * 4 + v] * mask[0, w, y * 4 + v].astype(F32)
                    table[(s * 4 + v) * 16 + d * 4 + j] = c

    rank = 0
    chosen = [0] * 8
    for d in range(nsector):
        home = (sector - d + 16) % 16
        valid = (sector + 16 - place[home]) % 16 < place[16 + home]
        place[32 + d] = jnp.where(valid, rank, 0)
        for j in range(7):
            chosen[j] = jnp.where(valid & (rank == j), d, chosen[j])
        rank = rank + valid.astype(jnp.int32)

    size_here = tiles[sector] * TROW
    before = (sector + nsector - 1) % nsector
    size_prev = jnp.where(sector > 0, tiles[before] * TROW, 0)

    def piece(d, k):
        return own[k] if d == 0 else rcv[d - 1, k]

    def assemble(s, k, rows_kept):
        arrived(k)
        for d in range(4):
            row0 = pl.multiple_of(((y + d) % 4) * 128, 128)
            v = piece(d, k).reshape(128, 512)
            i = lax.broadcasted_iota(jnp.int32, (128, 512), 0) + row0
            j = lax.broadcasted_iota(jnp.int32, (128, 512), 1)
            v = jnp.where((i < rows_kept) & (j < size_here), v, 0.0)
            t = v.T
            for h, (a, b) in enumerate(zip(halves(v), halves(t))):
                abuf[s * 2 + h, pl.ds(row0, 128), :] = a
                abuf[4 + s * 2 + h, :, pl.ds(row0, 128)] = b

    def f1(e):
        return remote(f1s.at[e], f1r.at[e], f1_send.at[e], f1_recv.at[e], above)

    def mix(k, nrows, put):
        arrived(k)

        def rows(r):
            span = pl.ds(pl.multiple_of(r * 8, 8), 8)
            acc = [None] * 8
            for d in range(4):
                for j in range(4):
                    x = own[k, j, span, :] if d == 0 else rcv[d - 1, k, j, span, :]
                    for o in range(8):
                        term = table[o * 16 + d * 4 + j] * x
                        acc[o] = term if acc[o] is None else acc[o] + term
            put(r, acc)

        loop(0, nrows // 8, rows)

    def mix_low(e):
        def put(r, acc):
            span = pl.ds(pl.multiple_of(r * 8, 8), 8)
            for v in range(4):
                f0[e, v, span, :] = acc[v]
                f1s[e, v, span, :] = acc[4 + v]

        mix(LOW[e], CH, put)
        f1(e).start()

    def mix_shared(n):
        def put(r, acc):
            span = pl.ds(pl.multiple_of((r % 2) * 8, 8), 8)
            for v in range(4):
                fu[0, 2 * n + r // 2, v, span, :] = acc[v]
                fu[1, 2 * n + r // 2, v, span, :] = acc[4 + v]

        mix(SHARED[n], UR if n == 3 else CH, put)

    back = (back0, back1)

    def give(s, d):
        source = pack if s == 0 else up
        to = ring(nsector - d + s)
        return remote(source.at[d], back[s].at[d], bk_send.at[s, d], bk_recv.at[s, d], to)

    def give_back():
        loop(1, nsector, lambda d: share(d).wait_send())
        back0[0] = fu[0, place[32]]
        back1[1] = fu[1, place[33]]

        def send(s, d):
            (pack if s == 0 else up)[d] = fu[s, place[32 + d]]
            give(s, d).start()

        send(1, 0)
        send(0, 1)

        def both(d):
            send(0, d)
            send(1, d)

        loop(2, nsector, both)

    def given(s):
        send_range = range(1, 2) if s == 0 else range(0, 1)
        for d in send_range:
            give(s, d).wait_recv()
        loop(2, nsector, lambda d: give(s, d).wait_recv())

    def store_h(group, s, r, count, rows, at):
        for h, part in enumerate(halves(r)):
            part = part.reshape(count, 4, rows, 512)
            for u in range(count):
                for v in range(4):
                    hbuf[group, s, h, v, pl.ds(pl.multiple_of(at + u * rows, 16), rows), :] = part[u, v]

    def first_low(s, g):
        def half(t):
            at = 4 * g + 2 * t
            lhs = (f0 if s == 0 else f1r)[pl.ds(at, 2)]
            ah, al = halves(lhs.reshape(256, 512))
            store_h(0, s, dot3(ah, al, abuf[s * 2], abuf[s * 2 + 1]), 2, CH, at * CH)

        loop(0, 2, half)

    def first_shared(s):
        home = sector if s == 0 else before

        def quarter(t):
            units = [back[s][(4 * t + i + place[home] + 16 - home) % 16] for i in range(4)]
            ah, al = halves(jnp.concatenate([u.reshape(64, 512) for u in units], axis=0))
            store_h(1, s, dot3(ah, al, abuf[s * 2], abuf[s * 2 + 1]), 4, UR, t * 64)

        loop(0, 4, quarter)

    def second(group, v):
        cols = pl.ds(group * 256, 256)
        r = None
        for s in range(2):
            t = dot3(abuf[4 + s * 2, :, cols], abuf[5 + s * 2, :, cols], hbuf[group, s, 0, v], hbuf[group, s, 1, v])
            r = t if r is None else r + t
        if group == 1:
            z[v] = r
        else:
            z[v] += r

    relay(0)
    issue(A0)
    relay(1)
    mix_low(0)
    relay(2)
    mix_low(1)
    loop(1, nsector, lambda d: share(d).wait_recv())
    for n in range(4):
        for t in range(1 if n == 3 else 2):
            own[SHARED[n], :, pl.ds(t * UR, UR), :] = got[chosen[2 * n + t]]
    issue(4)
    issue(5)
    relay(3)
    mix_low(2)
    issue(6)
    relay(4)
    assemble(0, A0, size_here)
    issue(7)
    relay(5)
    mix_shared(0)
    shift().wait_recv()
    issue(A1)
    relay(6)
    mix_shared(1)
    issue(9)
    relay(7)
    mix_shared(2)
    issue(10)
    relay(8)
    mix_shared(3)
    give_back()
    issue(11)
    relay(9)
    assemble(1, A1, size_prev)
    issue(12)
    relay(10)
    mix_low(3)
    issue(13)
    first_low(0, 0)
    relay(11)
    mix_low(4)
    issue(14)
    relay(12)
    mix_low(5)
    relay(13)
    mix_low(6)
    given(0)
    first_shared(0)
    relay(14)
    mix_low(7)
    first_low(0, 1)
    given(1)
    first_shared(1)
    loop(0, 4, lambda v: second(1, v))

    arrived(PSI)
    for d in range(4):
        row0 = pl.multiple_of(((y + d) % 4) * 128, 128)
        for h, part in enumerate(halves(piece(d, PSI).reshape(128, 512))):
            pbuf[h, pl.ds(row0, 128), :] = part

    for g in range(2):
        loop(4 * g, 4 * g + 4, lambda e: f1(e).wait_recv())
        first_low(1, g)

    def exchange(v):
        return remote(z.at[v], zp.at[v], zp_send.at[v], zp_recv.at[v], other)

    def out(v):
        return pltpu.make_async_copy(z.at[v], fresh.at[v], out_sem.at[v])

    def finish(v):
        second(0, v)
        exchange(v).start()
        out(v).start()

    loop(0, 4, finish)

    def apply_left(v):
        exchange(v).wait_recv()
        lh, ll = halves(jnp.where(section == 0, z[v], zp[v]))
        x = dot3(lh, ll, pbuf[0], pbuf[1]) * center[0, y * 4 + v]
        for h, part in enumerate(halves(x)):
            hbuf[0, 0, h, v] = part[:256]
            hbuf[0, 1, h, v] = part[256:]
        rh, rl = halves(jnp.where(section == 0, zp[v], z[v]))
        abuf[2 * v] = rh
        abuf[2 * v + 1] = rl

    loop(0, 4, apply_left)

    def partial(b):
        rows = pl.ds(pl.multiple_of((b % 2) * 128, 128), 128)
        r = None
        for v in range(4):
            t = dot3(hbuf[0, b // 2, 0, v, rows, :], hbuf[0, b // 2, 1, v, rows, :], abuf[2 * v], abuf[2 * v + 1])
            r = t if r is None else r + t
        return r

    hops = [
        remote(q.at[0, 0], s1.at[0], rs_send.at[0], rs_recv.at[0], right),
        remote(q.at[0, 1], s1.at[1], rs_send.at[1], rs_recv.at[1], left),
        remote(q.at[1], s2.at[0], rs_send.at[2], rs_recv.at[2], right),
        remote(q.at[2], s2.at[1], rs_send.at[3], rs_recv.at[3], left),
    ]

    def keep(slot, r):
        q[slot, 0] = r[:, :256]
        q[slot, 1] = r[:, 256:]

    keep(0, partial((y + 2) % 4))
    hops[0].start()
    hops[1].start()
    keep(1, partial((y + 1) % 4))
    hops[0].wait_recv()
    q[1, 0] += s1[0]
    hops[2].start()
    keep(2, partial((y + 3) % 4))
    hops[1].wait_recv()
    q[2, 1] += s1[1]
    hops[3].start()
    keep(3, partial(y))
    hops[2].wait_recv()
    hops[3].wait_recv()
    for t in range(2):
        hpsi[:, pl.ds(t * 256, 256)] = q[3, t] + (s2[0, t] + s2[1, t])

    for hop in hops:
        hop.wait_send()
    shift().wait_send()
    for k in range(NK):
        to_right(k).wait_send()
        to_left(k).wait_send()
        on_right(k).wait_send()
        on_left(k).wait_send()
    loop(0, NL, lambda e: f1(e).wait_send())
    give(1, 0).wait_send()
    give(0, 1).wait_send()

    def gone(d):
        give(0, d).wait_send()
        give(1, d).wait_send()

    loop(2, nsector, gone)

    def last(v):
        exchange(v).wait_send()
        out(v).wait()

    loop(0, 4, last)


def local(env, site, sector_tiles, mpo_mask, mpo_coef, psi, center_coef):
    spins = site[0].transpose(1, 0, 2).reshape(2, 4, CH, 512)
    anywhere = pl.BlockSpec(memory_space=pl.ANY)
    scalars = pl.BlockSpec(memory_space=pltpu.SMEM)
    dma = pltpu.SemaphoreType.DMA
    fresh, hpsi = pl.pallas_call(
        functools.partial(kernel, sector_tiles.shape[0]),
        out_shape=(
            jax.ShapeDtypeStruct((4, 512, 512), F32),
            jax.ShapeDtypeStruct((128, 512), F32),
        ),
        in_specs=[anywhere, anywhere, anywhere, scalars, scalars, scalars, scalars],
        out_specs=(anywhere, pl.BlockSpec(memory_space=pltpu.VMEM)),
        scratch_shapes=[
            pltpu.VMEM((NK, 4, CH, 512), F32),
            pltpu.VMEM((3, NK, 4, CH, 512), F32),
            pltpu.VMEM((NL, 4, CH, 512), F32),
            pltpu.VMEM((NL, 4, CH, 512), F32),
            pltpu.VMEM((NL, 4, CH, 512), F32),
            pltpu.VMEM((16, 4, UR, 512), F32),
            pltpu.VMEM((16, 4, UR, 512), F32),
            pltpu.VMEM((16, 4, UR, 512), F32),
            pltpu.VMEM((2, 7, 4, UR, 512), F32),
            pltpu.VMEM((16, 4, UR, 512), F32),
            pltpu.VMEM((16, 4, UR, 512), F32),
            pltpu.VMEM((2, 2, 2, 4, 256, 512), BF16),
            pltpu.VMEM((4, 512, 512), F32),
            pltpu.VMEM((4, 512, 512), F32),
            pltpu.VMEM((8, 512, 512), BF16),
            pltpu.VMEM((2, 512, 512), BF16),
            pltpu.VMEM((4, 2, 128, 256), F32),
            pltpu.VMEM((2, 128, 256), F32),
            pltpu.VMEM((2, 2, 128, 256), F32),
            pltpu.SMEM((128,), F32),
            pltpu.SMEM((48,), jnp.int32),
            dma((NK,)), dma((16,)), dma((2,)), dma((2, NK)), dma((2, NK)), dma((2, NK)), dma((2, NK)),
            dma((NL,)), dma((NL,)), dma((16,)), dma((16,)), dma((2, 16)), dma((2, 16)),
            dma((4,)), dma((4,)), dma((4,)), dma((4,)), dma((4,)),
        ],
        compiler_params=pltpu.CompilerParams(
            collective_id=0, has_side_effects=True, vmem_limit_bytes=62 << 20
        ),
        name="window",
    )(env[0], spins, psi[0].reshape(4, CH, 512), sector_tiles, mpo_mask, mpo_coef, center_coef)
    return fresh[None], hpsi[None]


def solution(mesh):
    placed = (
        P("section", "block", None, None),
        P("section", "block", None, None),
        P(),
        P("section", None, None),
        P("section", None, None, None),
        P("section", "block", None),
        P("section", None),
    )
    return jax.shard_map(
        local,
        mesh=mesh,
        in_specs=placed,
        out_specs=(P("section", "block", None, None), P("section", "block", None)),
        check_vma=False,
    )
```

```python
import functools

import jax
import jax.numpy as jnp
from jax import lax
from jax.experimental import pallas as pl
from jax.experimental.pallas import tpu as pltpu
from jax.sharding import PartitionSpec as P

TROW = 32
CH = 32
UR = 16
NL = 8
LOW = (0, 1, 2, 7, 9, 11, 12, 13)
A0, A1, PSI = 8, 10, 14
SHARED = (3, 4, 5, 6)
NK = 15
ORDER = (1, 4, 15, 12, 5, 11, 3, 13, 2, 8, 6, 9, 14, 7, 10)
MESH = pl.DeviceIdType.MESH
F32, BF16 = jnp.float32, jnp.bfloat16


def halves(value):
    high = value.astype(BF16)
    low = (value - high.astype(F32)).astype(BF16)
    return high, low


def dot3(ah, al, bh, bl):
    dot = functools.partial(jnp.dot, preferred_element_type=F32)
    return dot(ah, bh) + (dot(ah, bl) + dot(al, bh))


def kernel(nsector, env, site, psi, tiles, mask, coef, center, fresh, hpsi,
           own, rcv, f0, f1s, f1r, up, pack, got, fu, back0, back1, hbuf, z, zp, abuf, pbuf, q, s1, s2, table, place,
           load_sem, up_sem, shift_sem, own_send, own_recv, fwd_send, fwd_recv, f1_send, f1_recv,
           sh_send, sh_recv, bk_send, bk_recv, zp_send, zp_recv, out_sem, rs_send, rs_recv):
    section = lax.axis_index("section")
    block = lax.axis_index("block")
    sector = block // 4
    y = block % 4
    base = block - y
    right = (section, base + (y + 1) % 4)
    left = (section, base + (y + 3) % 4)
    other = (1 - section, block)

    def ring(distance):
        return (section, ((sector + distance + nsector) % nsector) * 4 + y)

    above = ring(1)

    def remote(src, dst, send, recv, to):
        return pltpu.make_async_remote_copy(
            src_ref=src, dst_ref=dst, send_sem=send, recv_sem=recv, device_id=to, device_id_type=MESH)

    def loop(lo, hi, body):
        lax.fori_loop(lo, hi, lambda i, c: (body(i), c)[1], 0)

    def load(k):
        if k == A0:
            src = site.at[0]
        elif k == PSI:
            src = psi
        else:
            src = env.at[:, pl.ds(LOW.index(k) * CH, CH), :]
        return pltpu.make_async_copy(src, own.at[k], load_sem.at[k])

    def load_up(u):
        rows = pl.ds(pl.multiple_of(256 + u * UR, UR), UR)
        return pltpu.make_async_copy(env.at[:, rows, :], up.at[u], up_sem.at[u])

    load(0).start()
    loop(0, nsector, lambda u: load_up(u).start())
    for k in LOW[1:] + (A0, PSI):
        load(k).start()

    barrier = pltpu.get_barrier_semaphore()
    for peer in (right, left, other):
        pl.semaphore_signal(barrier, inc=1, device_id=peer, device_id_type=MESH)
    loop(1, nsector, lambda d: pl.semaphore_signal(barrier, inc=1, device_id=ring(d), device_id_type=MESH))
    pl.semaphore_wait(barrier, nsector + 2)

    def shift():
        return remote(site.at[1], own.at[A1], shift_sem.at[0], shift_sem.at[1], above)

    def rows_of(k):
        return pl.ds(0, CH)

    def to_right(k):
        r = rows_of(k)
        return remote(own.at[k, :, r], rcv.at[2, k, :, r], own_send.at[0, k], own_recv.at[0, k], right)

    def to_left(k):
        r = rows_of(k)
        return remote(own.at[k, :, r], rcv.at[0, k, :, r], own_send.at[1, k], own_recv.at[1, k], left)

    def on_right(k):
        r = rows_of(k)
        return remote(rcv.at[2, k, pl.ds(0, 2), r], rcv.at[1, k, pl.ds(0, 2), r],
                      fwd_send.at[0, k], fwd_recv.at[0, k], right)

    def on_left(k):
        r = rows_of(k)
        return remote(rcv.at[0, k, pl.ds(2, 2), r], rcv.at[1, k, pl.ds(2, 2), r],
                      fwd_send.at[1, k], fwd_recv.at[1, k], left)

    def issue(k):
        if k in LOW + (A0, PSI):
            load(k).wait()
        to_right(k).start()
        to_left(k).start()

    def relay(k):
        to_right(k).wait_recv()
        on_right(k).start()
        to_left(k).wait_recv()
        on_left(k).start()

    def arrived(k):
        on_right(k).wait_recv()
        on_left(k).wait_recv()

    issue(0)

    start = 0
    for i in range(nsector):
        count = jnp.maximum(2 * (tiles[i] - 8), 0)
        place[i] = start % 16
        place[16 + i] = count
        start = start + count

    def share(d):
        return remote(pack.at[d], got.at[d], sh_send.at[d], sh_recv.at[d], ring(d))

    loop(0, nsector, lambda u: load_up(u).wait())

    def unit_for(d):
        return (sector + d + 16 - place[sector]) % 16

    got[0] = up[unit_for(0)]

    def send_share(d):
        pack[d] = up[unit_for(d)]
        share(d).start()

    for d in ORDER:
        send_share(d)
    shift().start()
    issue(1)
    issue(2)

    for s in range(2):
        for d in range(4):
            for j in range(4):
                w = ((y + d) % 4) * 4 + j
                for v in range(4):
                    c = coef[0, s, w, y * 4 + v] * mask[0, w, y * 4 + v].astype(F32)
                    table[(s * 4 + v) * 16 + d * 4 + j] = c

    rank = 0
    chosen = [0] * 8
    for d in range(nsector):
        home = (sector - d + 16) % 16
        valid = (sector + 16 - place[home]) % 16 < place[16 + home]
        place[32 + d] = jnp.where(valid, rank, 0)
        for j in range(7):
            chosen[j] = jnp.where(valid & (rank == j), d, chosen[j])
        rank = rank + valid.astype(jnp.int32)

    size_here = tiles[sector] * TROW
    before = (sector + nsector - 1) % nsector
    size_prev = jnp.where(sector > 0, tiles[before] * TROW, 0)

    def piece(d, k):
        return own[k] if d == 0 else rcv[d - 1, k]

    def assemble(s, k, rows_kept):
        arrived(k)
        for d in range(4):
            row0 = pl.multiple_of(((y + d) % 4) * 128, 128)
            v = piece(d, k).reshape(128, 512)
            i = lax.broadcasted_iota(jnp.int32, (128, 512), 0) + row0
            j = lax.broadcasted_iota(jnp.int32, (128, 512), 1)
            v = jnp.where((i < rows_kept) & (j < size_here), v, 0.0)
            t = v.T
            for h, (a, b) in enumerate(zip(halves(v), halves(t))):
                abuf[s * 2 + h, pl.ds(row0, 128), :] = a
                abuf[4 + s * 2 + h, :, pl.ds(row0, 128)] = b

    def f1(e):
        return remote(f1s.at[e], f1r.at[e], f1_send.at[e], f1_recv.at[e], above)

    def mix(k, nrows, put):
        arrived(k)

        def rows(r):
            span = pl.ds(pl.multiple_of(r * 8, 8), 8)
            acc = [None] * 8
            for d in range(4):
                for j in range(4):
                    x = own[k, j, span, :] if d == 0 else rcv[d - 1, k, j, span, :]
                    for o in range(8):
                        term = table[o * 16 + d * 4 + j] * x
                        acc[o] = term if acc[o] is None else acc[o] + term
            put(r, acc)

        loop(0, nrows // 8, rows)

    def mix_low(e):
        def put(r, acc):
            span = pl.ds(pl.multiple_of(r * 8, 8), 8)
            for v in range(4):
                f0[e, v, span, :] = acc[v]
                f1s[e, v, span, :] = acc[4 + v]

        mix(LOW[e], CH, put)
        f1(e).start()

    def mix_shared(n):
        def put(r, acc):
            span = pl.ds(pl.multiple_of((r % 2) * 8, 8), 8)
            for o in range(8):
                for c in range(2):
                    unit = n % 2 * 4 + 2 * c + r // 2
                    fu[n // 2, o // 4, unit, o % 4, span, :] = acc[o][:, c * 256:c * 256 + 256]

        mix(SHARED[n], CH, put)

    back = (back0, back1)

    def give(h, s, d):
        source = pack if s == 0 else up
        to = ring(nsector - d + s)
        cols = pl.ds(h * 256, 256)
        return remote(source.at[d, :, :, cols], back[s].at[d, :, :, cols], bk_send.at[h, s, d], bk_recv.at[h, s, d], to)

    def give_back(h):
        cols = pl.ds(h * 256, 256)
        if h == 0:
            loop(1, nsector, lambda d: share(d).wait_send())
        back0[0, :, :, cols] = fu[h, 0, place[32]]
        back1[1, :, :, cols] = fu[h, 1, place[33]]

        def send(s, d):
            (pack if s == 0 else up)[d, :, :, cols] = fu[h, s, place[32 + d]]
            give(h, s, d).start()

        for d in ORDER:
            send(0, 16 - d)
        for d in ORDER:
            send(1, (17 - d) % 16)

    def given(s):
        for h in range(2):
            give(h, s, 1 - s).wait_recv()
            loop(2, nsector, lambda d, h=h: give(h, s, d).wait_recv())

    def store_h(group, s, r, count, rows, at):
        for h, part in enumerate(halves(r)):
            part = part.reshape(count, 4, rows, 512)
            for u in range(count):
                for v in range(4):
                    hbuf[group, s, h, v, pl.ds(pl.multiple_of(at + u * rows, 16), rows), :] = part[u, v]

    def first_low(s, g):
        def half(t):
            at = 4 * g + 2 * t
            lhs = (f0 if s == 0 else f1r)[pl.ds(at, 2)]
            ah, al = halves(lhs.reshape(256, 512))
            store_h(0, s, dot3(ah, al, abuf[s * 2], abuf[s * 2 + 1]), 2, CH, at * CH)

        loop(0, 2, half)

    def first_shared(s):
        home = sector if s == 0 else before

        def quarter(t):
            units = [back[s][(4 * t + i + place[home] + 16 - home) % 16] for i in range(4)]
            ah, al = halves(jnp.concatenate([u.reshape(64, 512) for u in units], axis=0))
            store_h(1, s, dot3(ah, al, abuf[s * 2], abuf[s * 2 + 1]), 4, UR, t * 64)

        loop(0, 4, quarter)

    def second(group, v):
        cols = pl.ds(group * 256, 256)
        r = None
        for s in range(2):
            t = dot3(abuf[4 + s * 2, :, cols], abuf[5 + s * 2, :, cols], hbuf[group, s, 0, v], hbuf[group, s, 1, v])
            r = t if r is None else r + t
        if group == 0:
            z[v] = r
        else:
            z[v] += r

    relay(0)
    relay(1)
    mix_low(0)
    relay(2)
    mix_low(1)
    loop(1, nsector, lambda d: share(d).wait_recv())
    for n in range(4):
        for i in range(4):
            own[SHARED[n], :, pl.ds(i % 2 * UR, UR), pl.ds(i // 2 * 256, 256)] = got[
                chosen[n % 2 * 4 + i], :, :, pl.ds(n // 2 * 256, 256)]
    issue(3)
    issue(4)
    issue(5)
    mix_low(2)
    relay(3)
    issue(6)
    relay(4)
    mix_shared(0)
    issue(7)
    relay(5)
    mix_shared(1)
    issue(8)
    give_back(0)
    relay(6)
    mix_shared(2)
    issue(9)
    relay(7)
    mix_shared(3)
    give_back(1)
    shift().wait_recv()
    issue(10)
    relay(8)
    mix_low(3)
    issue(11)
    relay(9)
    assemble(0, A0, size_here)
    issue(12)
    relay(10)
    mix_low(4)
    issue(13)
    first_low(0, 0)
    relay(11)
    assemble(1, A1, size_prev)
    issue(14)
    relay(12)
    mix_low(5)
    relay(13)
    mix_low(6)
    given(0)
    first_shared(0)
    relay(14)
    mix_low(7)
    first_low(0, 1)
    arrived(PSI)
    for d in range(4):
        row0 = pl.multiple_of(((y + d) % 4) * 128, 128)
        for h, part in enumerate(halves(piece(d, PSI).reshape(128, 512))):
            pbuf[h, pl.ds(row0, 128), :] = part

    for g in range(2):
        loop(4 * g, 4 * g + 4, lambda e: f1(e).wait_recv())
        first_low(1, g)
    loop(0, 4, lambda v: second(0, v))
    given(1)
    first_shared(1)

    def exchange(v):
        return remote(z.at[v], zp.at[v], zp_send.at[v], zp_recv.at[v], other)

    def out(v):
        return pltpu.make_async_copy(z.at[v], fresh.at[v], out_sem.at[v])

    def finish(v):
        second(1, v)
        exchange(v).start()
        out(v).start()

    loop(0, 4, finish)

    def apply_left(v):
        exchange(v).wait_recv()
        lh, ll = halves(jnp.where(section == 0, z[v], zp[v]))
        x = dot3(lh, ll, pbuf[0], pbuf[1]) * center[0, y * 4 + v]
        for h, part in enumerate(halves(x)):
            hbuf[0, 0, h, v] = part[:256]
            hbuf[0, 1, h, v] = part[256:]
        rh, rl = halves(jnp.where(section == 0, zp[v], z[v]))
        abuf[2 * v] = rh
        abuf[2 * v + 1] = rl

    loop(0, 4, apply_left)

    def partial(b):
        rows = pl.ds(pl.multiple_of((b % 2) * 128, 128), 128)
        r = None
        for v in range(4):
            t = dot3(hbuf[0, b // 2, 0, v, rows, :], hbuf[0, b // 2, 1, v, rows, :], abuf[2 * v], abuf[2 * v + 1])
            r = t if r is None else r + t
        return r

    hops = [
        remote(q.at[0, 0], s1.at[0], rs_send.at[0], rs_recv.at[0], right),
        remote(q.at[0, 1], s1.at[1], rs_send.at[1], rs_recv.at[1], left),
        remote(q.at[1], s2.at[0], rs_send.at[2], rs_recv.at[2], right),
        remote(q.at[2], s2.at[1], rs_send.at[3], rs_recv.at[3], left),
    ]

    def keep(slot, r):
        q[slot, 0] = r[:, :256]
        q[slot, 1] = r[:, 256:]

    keep(0, partial((y + 2) % 4))
    hops[0].start()
    hops[1].start()
    keep(1, partial((y + 1) % 4))
    hops[0].wait_recv()
    q[1, 0] += s1[0]
    hops[2].start()
    keep(2, partial((y + 3) % 4))
    hops[1].wait_recv()
    q[2, 1] += s1[1]
    hops[3].start()
    keep(3, partial(y))
    hops[2].wait_recv()
    hops[3].wait_recv()
    for t in range(2):
        hpsi[:, pl.ds(t * 256, 256)] = q[3, t] + (s2[0, t] + s2[1, t])

    for hop in hops:
        hop.wait_send()
    shift().wait_send()
    for k in range(NK):
        to_right(k).wait_send()
        to_left(k).wait_send()
        on_right(k).wait_send()
        on_left(k).wait_send()
    loop(0, NL, lambda e: f1(e).wait_send())
    for h in range(2):
        for s in range(2):
            give(h, s, 1 - s).wait_send()
            loop(2, nsector, lambda d, h=h, s=s: give(h, s, d).wait_send())

    def last(v):
        exchange(v).wait_send()
        out(v).wait()

    loop(0, 4, last)


def settle(src, dst, held, came, gone):
    def part(ref, i):
        return ref.at[i // 4, pl.ds(i % 4 * 128, 128), :]

    incoming = [pltpu.make_async_copy(part(src, i), held.at[i], came.at[i]) for i in range(16)]
    outgoing = [pltpu.make_async_copy(held.at[i], part(dst, i), gone.at[i]) for i in range(16)]
    for copy in incoming:
        copy.start()
    for i in range(16):
        incoming[i].wait()
        outgoing[i].start()
    for copy in outgoing:
        copy.wait()


def local(env, site, sector_tiles, mpo_mask, mpo_coef, psi, center_coef):
    spins = site[0].transpose(1, 0, 2).reshape(2, 4, CH, 512)
    anywhere = pl.BlockSpec(memory_space=pl.ANY)
    scalars = pl.BlockSpec(memory_space=pltpu.SMEM)
    dma = pltpu.SemaphoreType.DMA
    fresh, hpsi = pl.pallas_call(
        functools.partial(kernel, sector_tiles.shape[0]),
        out_shape=(
            jax.ShapeDtypeStruct((4, 512, 512), F32),
            jax.ShapeDtypeStruct((128, 512), F32),
        ),
        in_specs=[anywhere, anywhere, anywhere, scalars, scalars, scalars, scalars],
        out_specs=(anywhere, pl.BlockSpec(memory_space=pltpu.VMEM)),
        scratch_shapes=[
            pltpu.VMEM((NK, 4, CH, 512), F32),
            pltpu.VMEM((3, NK, 4, CH, 512), F32),
            pltpu.VMEM((NL, 4, CH, 512), F32),
            pltpu.VMEM((NL, 4, CH, 512), F32),
            pltpu.VMEM((NL, 4, CH, 512), F32),
            pltpu.VMEM((16, 4, UR, 512), F32),
            pltpu.VMEM((16, 4, UR, 512), F32),
            pltpu.VMEM((16, 4, UR, 512), F32),
            pltpu.VMEM((2, 2, 8, 4, UR, 256), F32),
            pltpu.VMEM((16, 4, UR, 512), F32),
            pltpu.VMEM((16, 4, UR, 512), F32),
            pltpu.VMEM((2, 2, 2, 4, 256, 512), BF16),
            pltpu.VMEM((4, 512, 512), F32),
            pltpu.VMEM((4, 512, 512), F32),
            pltpu.VMEM((8, 512, 512), BF16),
            pltpu.VMEM((2, 512, 512), BF16),
            pltpu.VMEM((4, 2, 128, 256), F32),
            pltpu.VMEM((2, 128, 256), F32),
            pltpu.VMEM((2, 2, 128, 256), F32),
            pltpu.SMEM((128,), F32),
            pltpu.SMEM((48,), jnp.int32),
            dma((NK,)), dma((16,)), dma((2,)), dma((2, NK)), dma((2, NK)), dma((2, NK)), dma((2, NK)),
            dma((NL,)), dma((NL,)), dma((16,)), dma((16,)), dma((2, 2, 16)), dma((2, 2, 16)),
            dma((4,)), dma((4,)), dma((4,)), dma((4,)), dma((4,)),
        ],
        compiler_params=pltpu.CompilerParams(
            collective_id=0, has_side_effects=True, vmem_limit_bytes=62 << 20
        ),
        name="window",
    )(env[0], spins, psi[0].reshape(4, CH, 512), sector_tiles, mpo_mask, mpo_coef, center_coef)
    fresh = pl.pallas_call(
        settle,
        out_shape=jax.ShapeDtypeStruct((4, 512, 512), F32),
        in_specs=[anywhere],
        out_specs=anywhere,
        scratch_shapes=[pltpu.VMEM((16, 128, 512), F32), dma((16,)), dma((16,))],
        name="settle",
    )(fresh)
    return fresh[None], hpsi[None]


def solution(mesh):
    placed = (
        P("section", "block", None, None),
        P("section", "block", None, None),
        P(),
        P("section", None, None),
        P("section", None, None, None),
        P("section", "block", None),
        P("section", None),
    )
    return jax.shard_map(
        local,
        mesh=mesh,
        in_specs=placed,
        out_specs=(P("section", "block", None, None), P("section", "block", None)),
        check_vma=False,
    )
```

```python
import functools

import jax
import jax.numpy as jnp
from jax import lax
from jax.experimental import pallas as pl
from jax.experimental.pallas import tpu as pltpu
from jax.sharding import PartitionSpec as P

TROW = 32
CH = 32
UR = 16
NL = 8
LOW = (0, 1, 2, 7, 9, 11, 12, 13)
A0, A1, PSI = 8, 10, 14
SHARED = (3, 4, 5, 6)
NK = 15
ORDER = (1, 4, 15, 12, 5, 11, 3, 13, 2, 8, 6, 9, 14, 7, 10)
MESH = pl.DeviceIdType.MESH
F32, BF16 = jnp.float32, jnp.bfloat16


def halves(value):
    high = value.astype(BF16)
    low = (value - high.astype(F32)).astype(BF16)
    return high, low


def dot3(ah, al, bh, bl):
    dot = functools.partial(jnp.dot, preferred_element_type=F32)
    return dot(ah, bh) + (dot(ah, bl) + dot(al, bh))


def kernel(nsector, env, site, psi, tiles, mask, coef, center, fresh, hpsi,
           own, rcv, f0, f1s, f1r, up, pack, got, fu, back0, back1, hbuf, z, zp, abuf, pbuf, stage, total, q, s1, s2, table, place,
           load_sem, up_sem, shift_sem, own_send, own_recv, fwd_send, fwd_recv, f1_send, f1_recv,
           sh_send, sh_recv, bk_send, bk_recv, zp_send, zp_recv, out_sem, rs_send, rs_recv):
    section = lax.axis_index("section")
    block = lax.axis_index("block")
    sector = block // 4
    y = block % 4
    base = block - y
    right = (section, base + (y + 1) % 4)
    left = (section, base + (y + 3) % 4)
    other = (1 - section, block)

    def ring(distance):
        return (section, ((sector + distance + nsector) % nsector) * 4 + y)

    above = ring(1)

    def remote(src, dst, send, recv, to):
        return pltpu.make_async_remote_copy(
            src_ref=src, dst_ref=dst, send_sem=send, recv_sem=recv, device_id=to, device_id_type=MESH)

    def loop(lo, hi, body):
        lax.fori_loop(lo, hi, lambda i, c: (body(i), c)[1], 0)

    def load(k):
        if k == PSI:
            src = psi
        else:
            src = env.at[:, pl.ds(LOW.index(k) * CH, CH), :]
        return pltpu.make_async_copy(src, own.at[k], load_sem.at[k])

    def load_up(u):
        rows = pl.ds(pl.multiple_of(256 + u * UR, UR), UR)
        return pltpu.make_async_copy(env.at[:, rows, :], up.at[u], up_sem.at[u])

    load(0).start()
    loop(0, nsector, lambda u: load_up(u).start())
    for k in LOW[1:] + (PSI,):
        load(k).start()

    barrier = pltpu.get_barrier_semaphore()
    for peer in (right, left, other):
        pl.semaphore_signal(barrier, inc=1, device_id=peer, device_id_type=MESH)
    loop(1, nsector, lambda d: pl.semaphore_signal(barrier, inc=1, device_id=ring(d), device_id_type=MESH))
    pl.semaphore_wait(barrier, nsector + 2)

    def shift():
        return remote(stage, own.at[A1], shift_sem.at[0], shift_sem.at[1], above)

    def rows_of(k):
        return pl.ds(0, CH)

    def to_right(k):
        r = rows_of(k)
        return remote(own.at[k, :, r], rcv.at[2, k, :, r], own_send.at[0, k], own_recv.at[0, k], right)

    def to_left(k):
        r = rows_of(k)
        return remote(own.at[k, :, r], rcv.at[0, k, :, r], own_send.at[1, k], own_recv.at[1, k], left)

    def on_right(k):
        r = rows_of(k)
        return remote(rcv.at[2, k, pl.ds(0, 2), r], rcv.at[1, k, pl.ds(0, 2), r],
                      fwd_send.at[0, k], fwd_recv.at[0, k], right)

    def on_left(k):
        r = rows_of(k)
        return remote(rcv.at[0, k, pl.ds(2, 2), r], rcv.at[1, k, pl.ds(2, 2), r],
                      fwd_send.at[1, k], fwd_recv.at[1, k], left)

    def issue(k):
        if k in LOW + (PSI,):
            load(k).wait()
        to_right(k).start()
        to_left(k).start()

    def relay(k):
        to_right(k).wait_recv()
        on_right(k).start()
        to_left(k).wait_recv()
        on_left(k).start()

    def arrived(k):
        on_right(k).wait_recv()
        on_left(k).wait_recv()

    issue(0)

    start = 0
    for i in range(nsector):
        count = jnp.maximum(2 * (tiles[i] - 8), 0)
        place[i] = start % 16
        place[16 + i] = count
        start = start + count

    def share(d):
        return remote(pack.at[d], got.at[d], sh_send.at[d], sh_recv.at[d], ring(d))

    loop(0, nsector, lambda u: load_up(u).wait())

    def unit_for(d):
        return (sector + d + 16 - place[sector]) % 16

    got[0] = up[unit_for(0)]

    def send_share(d):
        pack[d] = up[unit_for(d)]
        share(d).start()

    for d in ORDER:
        send_share(d)
    issue(1)
    issue(2)
    own[A0] = site[:, 0, :].reshape(4, CH, 512)
    stage[...] = site[:, 1, :].reshape(4, CH, 512)

    for s in range(2):
        for d in range(4):
            for j in range(4):
                w = ((y + d) % 4) * 4 + j
                for v in range(4):
                    c = coef[0, s, w, y * 4 + v] * mask[0, w, y * 4 + v].astype(F32)
                    table[(s * 4 + v) * 16 + d * 4 + j] = c

    rank = 0
    chosen = [0] * 8
    for d in range(nsector):
        home = (sector - d + 16) % 16
        valid = (sector + 16 - place[home]) % 16 < place[16 + home]
        place[32 + d] = jnp.where(valid, rank, 0)
        for j in range(7):
            chosen[j] = jnp.where(valid & (rank == j), d, chosen[j])
        rank = rank + valid.astype(jnp.int32)

    size_here = tiles[sector] * TROW
    before = (sector + nsector - 1) % nsector
    size_prev = jnp.where(sector > 0, tiles[before] * TROW, 0)

    def piece(d, k):
        return own[k] if d == 0 else rcv[d - 1, k]

    def assemble(s, k, rows_kept):
        arrived(k)
        for d in range(4):
            row0 = pl.multiple_of(((y + d) % 4) * 128, 128)
            v = piece(d, k).reshape(128, 512)
            i = lax.broadcasted_iota(jnp.int32, (128, 512), 0) + row0
            j = lax.broadcasted_iota(jnp.int32, (128, 512), 1)
            v = jnp.where((i < rows_kept) & (j < size_here), v, 0.0)
            t = v.T
            for h, (a, b) in enumerate(zip(halves(v), halves(t))):
                abuf[s * 2 + h, pl.ds(row0, 128), :] = a
                abuf[4 + s * 2 + h, :, pl.ds(row0, 128)] = b

    def f1(e):
        return remote(f1s.at[e], f1r.at[e], f1_send.at[e], f1_recv.at[e], above)

    def mix(k, nrows, put):
        arrived(k)

        def rows(r):
            span = pl.ds(pl.multiple_of(r * 8, 8), 8)
            acc = [None] * 8
            for d in range(4):
                for j in range(4):
                    x = own[k, j, span, :] if d == 0 else rcv[d - 1, k, j, span, :]
                    for o in range(8):
                        term = table[o * 16 + d * 4 + j] * x
                        acc[o] = term if acc[o] is None else acc[o] + term
            put(r, acc)

        loop(0, nrows // 8, rows)

    def mix_low(e, send=True):
        def put(r, acc):
            span = pl.ds(pl.multiple_of(r * 8, 8), 8)
            for v in range(4):
                f0[e, v, span, :] = acc[v]
                f1s[e, v, span, :] = acc[4 + v]

        mix(LOW[e], CH, put)
        if send:
            f1(e).start()

    def mix_shared(n):
        def put(r, acc):
            span = pl.ds(pl.multiple_of((r % 2) * 8, 8), 8)
            for o in range(8):
                for c in range(2):
                    unit = n % 2 * 4 + 2 * c + r // 2
                    fu[n // 2, o // 4, unit, o % 4, span, :] = acc[o][:, c * 256:c * 256 + 256]

        mix(SHARED[n], CH, put)

    back = (back0, back1)

    def give(h, s, d):
        source = pack if s == 0 else up
        to = ring(nsector - d + s)
        cols = pl.ds(h * 256, 256)
        return remote(source.at[d, :, :, cols], back[s].at[d, :, :, cols], bk_send.at[h, s, d], bk_recv.at[h, s, d], to)

    def give_back(h):
        cols = pl.ds(h * 256, 256)
        if h == 0:
            loop(1, nsector, lambda d: share(d).wait_send())
        back0[0, :, :, cols] = fu[h, 0, place[32]]
        back1[1, :, :, cols] = fu[h, 1, place[33]]

        def send(s, d):
            (pack if s == 0 else up)[d, :, :, cols] = fu[h, s, place[32 + d]]
            give(h, s, d).start()

        for d in ORDER:
            send(0, 16 - d)
        for d in ORDER:
            send(1, (17 - d) % 16)

    def given(s):
        for h in range(2):
            give(h, s, 1 - s).wait_recv()
            loop(2, nsector, lambda d, h=h: give(h, s, d).wait_recv())

    def store_h(group, s, r, count, rows, at):
        for h, part in enumerate(halves(r)):
            part = part.reshape(count, 4, rows, 512)
            for u in range(count):
                for v in range(4):
                    hbuf[group, s, h, v, pl.ds(pl.multiple_of(at + u * rows, 16), rows), :] = part[u, v]

    def first_low(s, g):
        def half(t):
            at = 4 * g + 2 * t
            lhs = (f0 if s == 0 else f1r)[pl.ds(at, 2)]
            ah, al = halves(lhs.reshape(256, 512))
            store_h(0, s, dot3(ah, al, abuf[s * 2], abuf[s * 2 + 1]), 2, CH, at * CH)

        loop(0, 2, half)

    def first_shared(s):
        home = sector if s == 0 else before

        def quarter(t):
            units = [back[s][(4 * t + i + place[home] + 16 - home) % 16] for i in range(4)]
            ah, al = halves(jnp.concatenate([u.reshape(64, 512) for u in units], axis=0))
            store_h(1, s, dot3(ah, al, abuf[s * 2], abuf[s * 2 + 1]), 4, UR, t * 64)

        loop(0, 4, quarter)

    def second(group, v):
        cols = pl.ds(group * 256, 256)
        r = None
        for s in range(2):
            t = dot3(abuf[4 + s * 2, :, cols], abuf[5 + s * 2, :, cols], hbuf[group, s, 0, v], hbuf[group, s, 1, v])
            r = t if r is None else r + t
        if group == 0:
            z[v] = r
        else:
            z[v] += r

    relay(0)
    relay(1)
    mix_low(0, send=False)
    relay(2)
    mix_low(1, send=False)
    loop(1, nsector, lambda d: share(d).wait_recv())
    for n in range(4):
        for i in range(4):
            own[SHARED[n], :, pl.ds(i % 2 * UR, UR), pl.ds(i // 2 * 256, 256)] = got[
                chosen[n % 2 * 4 + i], :, :, pl.ds(n // 2 * 256, 256)]
    issue(3)
    issue(4)
    issue(5)
    f1(0).start()
    f1(1).start()
    shift().start()
    mix_low(2)
    relay(3)
    issue(6)
    relay(4)
    mix_shared(0)
    issue(7)
    relay(5)
    mix_shared(1)
    issue(8)
    give_back(0)
    relay(6)
    mix_shared(2)
    issue(9)
    relay(7)
    mix_shared(3)
    give_back(1)
    shift().wait_recv()
    issue(10)
    relay(8)
    mix_low(3)
    issue(11)
    relay(9)
    assemble(0, A0, size_here)
    issue(12)
    relay(10)
    mix_low(4)
    issue(13)
    first_low(0, 0)
    relay(11)
    assemble(1, A1, size_prev)
    issue(14)
    relay(12)
    mix_low(5)
    relay(13)
    mix_low(6)
    given(0)
    first_shared(0)
    relay(14)
    mix_low(7)
    first_low(0, 1)
    arrived(PSI)
    for d in range(4):
        row0 = pl.multiple_of(((y + d) % 4) * 128, 128)
        for h, part in enumerate(halves(piece(d, PSI).reshape(128, 512))):
            pbuf[h, pl.ds(row0, 128), :] = part

    for g in range(2):
        loop(4 * g, 4 * g + 4, lambda e: f1(e).wait_recv())
        first_low(1, g)
    loop(0, 4, lambda v: second(0, v))
    given(1)
    first_shared(1)

    def exchange(v):
        return remote(z.at[v], zp.at[v], zp_send.at[v], zp_recv.at[v], other)

    def out(v):
        return pltpu.make_async_copy(z.at[v], fresh.at[v], out_sem.at[v])

    def finish(v):
        second(1, v)
        exchange(v).start()
        out(v).start()

    loop(0, 4, finish)

    def apply_left(v):
        exchange(v).wait_recv()
        lh, ll = halves(jnp.where(section == 0, z[v], zp[v]))
        x = dot3(lh, ll, pbuf[0], pbuf[1]) * center[0, y * 4 + v]
        return halves(x), halves(jnp.where(section == 0, zp[v], z[v]))

    total[...] = jnp.zeros_like(total)

    def add(v):
        (xh, xl), (rh, rl) = apply_left(v)
        total[...] += dot3(xh, xl, rh, rl)

    loop(0, 3, add)
    for h, (x, r) in enumerate(zip(*apply_left(3))):
        hbuf[0, 0, h, 0] = x[:256]
        hbuf[0, 1, h, 0] = x[256:]
        abuf[h] = r

    def partial(slot, b):
        rows = pl.ds(pl.multiple_of((b % 2) * 128, 128), 128)
        r = dot3(hbuf[0, b // 2, 0, 0, rows, :], hbuf[0, b // 2, 1, 0, rows, :], abuf[0], abuf[1])
        r += total[pl.ds(pl.multiple_of(b * 128, 128), 128), :]
        q[slot, 0] = r[:, :256]
        q[slot, 1] = r[:, 256:]

    hops = [
        remote(src, dst, rs_send.at[i], rs_recv.at[i], to) for i, (src, dst, to) in enumerate((
            (q.at[0, 0], s1.at[0], right),
            (q.at[0, 1], s1.at[1], left),
            (q.at[1, 1], s2.at[0, 1], right),
            (q.at[2, 0], s2.at[1, 0], left),
            (q.at[1, 0], s2.at[0, 0], right),
            (q.at[2, 1], s2.at[1, 1], left),
        ))
    ]

    partial(0, (y + 2) % 4)
    hops[0].start()
    hops[1].start()
    partial(1, (y + 1) % 4)
    hops[2].start()
    partial(2, (y + 3) % 4)
    hops[3].start()
    hops[0].wait_recv()
    q[1, 0] += s1[0]
    hops[4].start()
    hops[1].wait_recv()
    q[2, 1] += s1[1]
    hops[5].start()
    partial(3, y)
    for i in range(2, 6):
        hops[i].wait_recv()
    for t in range(2):
        hpsi[:, pl.ds(t * 256, 256)] = q[3, t] + (s2[0, t] + s2[1, t])

    for hop in hops:
        hop.wait_send()
    shift().wait_send()
    for k in range(NK):
        to_right(k).wait_send()
        to_left(k).wait_send()
        on_right(k).wait_send()
        on_left(k).wait_send()
    loop(0, NL, lambda e: f1(e).wait_send())
    for h in range(2):
        for s in range(2):
            give(h, s, 1 - s).wait_send()
            loop(2, nsector, lambda d, h=h, s=s: give(h, s, d).wait_send())

    def last(v):
        exchange(v).wait_send()
        out(v).wait()

    loop(0, 4, last)


def settle(src, dst, held, came, gone):
    def part(ref, i):
        return ref.at[i // 4, pl.ds(i % 4 * 128, 128), :]

    incoming = [pltpu.make_async_copy(part(src, i), held.at[i], came.at[i]) for i in range(16)]
    outgoing = [pltpu.make_async_copy(held.at[i], part(dst, i), gone.at[i]) for i in range(16)]
    for copy in incoming:
        copy.start()
    for i in range(16):
        incoming[i].wait()
        outgoing[i].start()
    for copy in outgoing:
        copy.wait()


def local(env, site, sector_tiles, mpo_mask, mpo_coef, psi, center_coef):
    anywhere = pl.BlockSpec(memory_space=pl.ANY)
    scalars = pl.BlockSpec(memory_space=pltpu.SMEM)
    dma = pltpu.SemaphoreType.DMA
    fresh, hpsi = pl.pallas_call(
        functools.partial(kernel, sector_tiles.shape[0]),
        out_shape=(
            jax.ShapeDtypeStruct((4, 512, 512), F32),
            jax.ShapeDtypeStruct((128, 512), F32),
        ),
        in_specs=[anywhere, pl.BlockSpec(memory_space=pltpu.VMEM), anywhere, scalars, scalars, scalars, scalars],
        out_specs=(anywhere, pl.BlockSpec(memory_space=pltpu.VMEM)),
        scratch_shapes=[
            pltpu.VMEM((NK, 4, CH, 512), F32),
            pltpu.VMEM((3, NK, 4, CH, 512), F32),
            pltpu.VMEM((NL, 4, CH, 512), F32),
            pltpu.VMEM((NL, 4, CH, 512), F32),
            pltpu.VMEM((NL, 4, CH, 512), F32),
            pltpu.VMEM((16, 4, UR, 512), F32),
            pltpu.VMEM((16, 4, UR, 512), F32),
            pltpu.VMEM((16, 4, UR, 512), F32),
            pltpu.VMEM((2, 2, 8, 4, UR, 256), F32),
            pltpu.VMEM((16, 4, UR, 512), F32),
            pltpu.VMEM((16, 4, UR, 512), F32),
            pltpu.VMEM((2, 2, 2, 4, 256, 512), BF16),
            pltpu.VMEM((4, 512, 512), F32),
            pltpu.VMEM((4, 512, 512), F32),
            pltpu.VMEM((8, 512, 512), BF16),
            pltpu.VMEM((2, 512, 512), BF16),
            pltpu.VMEM((4, CH, 512), F32),
            pltpu.VMEM((512, 512), F32),
            pltpu.VMEM((4, 2, 128, 256), F32),
            pltpu.VMEM((2, 128, 256), F32),
            pltpu.VMEM((2, 2, 128, 256), F32),
            pltpu.SMEM((128,), F32),
            pltpu.SMEM((48,), jnp.int32),
            dma((NK,)), dma((16,)), dma((2,)), dma((2, NK)), dma((2, NK)), dma((2, NK)), dma((2, NK)),
            dma((NL,)), dma((NL,)), dma((16,)), dma((16,)), dma((2, 2, 16)), dma((2, 2, 16)),
            dma((4,)), dma((4,)), dma((4,)), dma((6,)), dma((6,)),
        ],
        compiler_params=pltpu.CompilerParams(
            collective_id=0, has_side_effects=True, vmem_limit_bytes=62 << 20
        ),
        name="window",
    )(env[0], site[0], psi[0].reshape(4, CH, 512), sector_tiles, mpo_mask, mpo_coef, center_coef)
    fresh = pl.pallas_call(
        settle,
        out_shape=jax.ShapeDtypeStruct((4, 512, 512), F32),
        in_specs=[anywhere],
        out_specs=anywhere,
        scratch_shapes=[pltpu.VMEM((16, 128, 512), F32), dma((16,)), dma((16,))],
        name="settle",
    )(fresh)
    return fresh[None], hpsi[None]


def solution(mesh):
    placed = (
        P("section", "block", None, None),
        P("section", "block", None, None),
        P(),
        P("section", None, None),
        P("section", None, None, None),
        P("section", "block", None),
        P("section", None),
    )
    return jax.shard_map(
        local,
        mesh=mesh,
        in_specs=placed,
        out_specs=(P("section", "block", None, None), P("section", "block", None)),
        check_vma=False,
    )
```

```python
import functools

import jax
import jax.numpy as jnp
from jax import lax
from jax.experimental import pallas as pl
from jax.experimental.pallas import tpu as pltpu
from jax.sharding import PartitionSpec as P

TROW = 32
CH = 32
UR = 16
NL = 8
LOW = (0, 1, 2, 7, 9, 11, 12, 13)
A0, A1, PSI = 8, 10, 14
SHARED = (3, 4, 5, 6)
NK = 15
ORDER = (1, 4, 15, 12, 5, 11, 3, 13, 2, 8, 6, 9, 14, 7, 10)
MESH = pl.DeviceIdType.MESH
F32, BF16 = jnp.float32, jnp.bfloat16


def halves(value):
    high = value.astype(BF16)
    low = (value - high.astype(F32)).astype(BF16)
    return high, low


def dot3(ah, al, bh, bl):
    dot = functools.partial(jnp.dot, preferred_element_type=F32)
    return dot(ah, bh) + (dot(ah, bl) + dot(al, bh))


def kernel(nsector, env, site, psi, tiles, mask, coef, center, fresh, hpsi,
           own, rcv, f0, f1s, f1r, up, pack, got, fu, back0, back1, hbuf, z, zp, abuf, pbuf, stage, total, q, s1, s2, table, place,
           load_sem, up_sem, shift_sem, own_send, own_recv, fwd_send, fwd_recv, f1_send, f1_recv,
           sh_send, sh_recv, bk_send, bk_recv, zp_send, zp_recv, out_sem, rs_send, rs_recv):
    section = lax.axis_index("section")
    block = lax.axis_index("block")
    sector = block // 4
    y = block % 4
    base = block - y
    right = (section, base + (y + 1) % 4)
    left = (section, base + (y + 3) % 4)
    other = (1 - section, block)

    def ring(distance):
        return (section, ((sector + distance + nsector) % nsector) * 4 + y)

    above = ring(1)

    def remote(src, dst, send, recv, to):
        return pltpu.make_async_remote_copy(
            src_ref=src, dst_ref=dst, send_sem=send, recv_sem=recv, device_id=to, device_id_type=MESH)

    def loop(lo, hi, body):
        lax.fori_loop(lo, hi, lambda i, c: (body(i), c)[1], 0)

    def load(k):
        if k == PSI:
            src = psi
        else:
            src = env.at[:, pl.ds(LOW.index(k) * CH, CH), :]
        return pltpu.make_async_copy(src, own.at[k], load_sem.at[k])

    def load_up(u):
        rows = pl.ds(pl.multiple_of(256 + u * UR, UR), UR)
        return pltpu.make_async_copy(env.at[:, rows, :], up.at[u], up_sem.at[u])

    load(0).start()
    loop(0, nsector, lambda u: load_up(u).start())
    for k in LOW[1:] + (PSI,):
        load(k).start()

    barrier = pltpu.get_barrier_semaphore()
    for peer in (right, left, other):
        pl.semaphore_signal(barrier, inc=1, device_id=peer, device_id_type=MESH)
    loop(1, nsector, lambda d: pl.semaphore_signal(barrier, inc=1, device_id=ring(d), device_id_type=MESH))
    pl.semaphore_wait(barrier, nsector + 2)

    def shift():
        return remote(stage, own.at[A1], shift_sem.at[0], shift_sem.at[1], above)

    def rows_of(k):
        return pl.ds(0, CH)

    def to_right(k):
        r = rows_of(k)
        return remote(own.at[k, :, r], rcv.at[2, k, :, r], own_send.at[0, k], own_recv.at[0, k], right)

    def to_left(k):
        r = rows_of(k)
        return remote(own.at[k, :, r], rcv.at[0, k, :, r], own_send.at[1, k], own_recv.at[1, k], left)

    def on_right(k):
        r = rows_of(k)
        return remote(rcv.at[2, k, pl.ds(0, 2), r], rcv.at[1, k, pl.ds(0, 2), r],
                      fwd_send.at[0, k], fwd_recv.at[0, k], right)

    def on_left(k):
        r = rows_of(k)
        return remote(rcv.at[0, k, pl.ds(2, 2), r], rcv.at[1, k, pl.ds(2, 2), r],
                      fwd_send.at[1, k], fwd_recv.at[1, k], left)

    def issue(k):
        if k in LOW + (PSI,):
            load(k).wait()
        to_right(k).start()
        to_left(k).start()

    def relay(k):
        to_right(k).wait_recv()
        on_right(k).start()
        to_left(k).wait_recv()
        on_left(k).start()

    def arrived(k):
        on_right(k).wait_recv()
        on_left(k).wait_recv()

    issue(0)

    start = 0
    for i in range(nsector):
        count = jnp.maximum(2 * (tiles[i] - 8), 0)
        place[i] = start % 16
        place[16 + i] = count
        start = start + count

    def share(d):
        return remote(pack.at[d], got.at[d], sh_send.at[d], sh_recv.at[d], ring(d))

    loop(0, nsector, lambda u: load_up(u).wait())

    def unit_for(d):
        return (sector + d + 16 - place[sector]) % 16

    got[0] = up[unit_for(0)]

    def send_share(d):
        pack[d] = up[unit_for(d)]
        share(d).start()

    for d in ORDER:
        send_share(d)
    issue(1)
    issue(2)
    own[A0] = site[:, 0, :].reshape(4, CH, 512)
    stage[...] = site[:, 1, :].reshape(4, CH, 512)

    for s in range(2):
        for d in range(4):
            for j in range(4):
                w = ((y + d) % 4) * 4 + j
                for v in range(4):
                    c = coef[0, s, w, y * 4 + v] * mask[0, w, y * 4 + v].astype(F32)
                    table[(s * 4 + v) * 16 + d * 4 + j] = c

    rank = 0
    chosen = [0] * 8
    for d in range(nsector):
        home = (sector - d + 16) % 16
        valid = (sector + 16 - place[home]) % 16 < place[16 + home]
        place[32 + d] = jnp.where(valid, rank, 0)
        for j in range(7):
            chosen[j] = jnp.where(valid & (rank == j), d, chosen[j])
        rank = rank + valid.astype(jnp.int32)

    size_here = tiles[sector] * TROW
    before = (sector + nsector - 1) % nsector
    size_prev = jnp.where(sector > 0, tiles[before] * TROW, 0)

    def piece(d, k):
        return own[k] if d == 0 else rcv[d - 1, k]

    def assemble(s, k, rows_kept):
        arrived(k)
        for d in range(4):
            row0 = pl.multiple_of(((y + d) % 4) * 128, 128)
            v = piece(d, k).reshape(128, 512)
            i = lax.broadcasted_iota(jnp.int32, (128, 512), 0) + row0
            j = lax.broadcasted_iota(jnp.int32, (128, 512), 1)
            v = jnp.where((i < rows_kept) & (j < size_here), v, 0.0)
            t = v.T
            for h, (a, b) in enumerate(zip(halves(v), halves(t))):
                abuf[s * 2 + h, pl.ds(row0, 128), :] = a
                abuf[4 + s * 2 + h, :, pl.ds(row0, 128)] = b

    def f1(e):
        return remote(f1s.at[e], f1r.at[e], f1_send.at[e], f1_recv.at[e], above)

    def mix(k, nrows, put):
        arrived(k)

        def rows(r):
            span = pl.ds(pl.multiple_of(r * 8, 8), 8)
            acc = [None] * 8
            for d in range(4):
                for j in range(4):
                    x = own[k, j, span, :] if d == 0 else rcv[d - 1, k, j, span, :]
                    for o in range(8):
                        term = table[o * 16 + d * 4 + j] * x
                        acc[o] = term if acc[o] is None else acc[o] + term
            put(r, acc)

        loop(0, nrows // 8, rows)

    def mix_low(e, send=True):
        def put(r, acc):
            span = pl.ds(pl.multiple_of(r * 8, 8), 8)
            for v in range(4):
                f0[e, v, span, :] = acc[v]
                f1s[e, v, span, :] = acc[4 + v]

        mix(LOW[e], CH, put)
        if send:
            f1(e).start()

    def mix_shared(n):
        def put(r, acc):
            span = pl.ds(pl.multiple_of((r % 2) * 8, 8), 8)
            for o in range(8):
                for c in range(2):
                    unit = n % 2 * 4 + 2 * c + r // 2
                    fu[n // 2, o // 4, unit, o % 4, span, :] = acc[o][:, c * 256:c * 256 + 256]

        mix(SHARED[n], CH, put)

    back = (back0, back1)

    def give(h, s, d):
        source = pack if s == 0 else up
        to = ring(nsector - d + s)
        cols = pl.ds(h * 256, 256)
        return remote(source.at[d, :, :, cols], back[s].at[d, :, :, cols], bk_send.at[h, s, d], bk_recv.at[h, s, d], to)

    def give_back(h):
        cols = pl.ds(h * 256, 256)
        if h == 0:
            loop(1, nsector, lambda d: share(d).wait_send())
        back0[0, :, :, cols] = fu[h, 0, place[32]]
        back1[1, :, :, cols] = fu[h, 1, place[33]]

        def send(s, d):
            (pack if s == 0 else up)[d, :, :, cols] = fu[h, s, place[32 + d]]
            give(h, s, d).start()

        for d in ORDER:
            send(0, 16 - d)
        for d in ORDER:
            send(1, (17 - d) % 16)

    def given(s):
        for h in range(2):
            give(h, s, 1 - s).wait_recv()
            loop(2, nsector, lambda d, h=h: give(h, s, d).wait_recv())

    def store_h(group, s, r, count, rows, at):
        for h, part in enumerate(halves(r)):
            part = part.reshape(count, 4, rows, 512)
            for u in range(count):
                for v in range(4):
                    hbuf[group, s, h, v, pl.ds(pl.multiple_of(at + u * rows, 16), rows), :] = part[u, v]

    def first_low(s, g):
        def half(t):
            at = 4 * g + 2 * t
            lhs = (f0 if s == 0 else f1r)[pl.ds(at, 2)]
            ah, al = halves(lhs.reshape(256, 512))
            store_h(0, s, dot3(ah, al, abuf[s * 2], abuf[s * 2 + 1]), 2, CH, at * CH)

        loop(0, 2, half)

    def first_shared(s):
        home = sector if s == 0 else before

        def quarter(t):
            units = [back[s][(4 * t + i + place[home] + 16 - home) % 16] for i in range(4)]
            ah, al = halves(jnp.concatenate([u.reshape(64, 512) for u in units], axis=0))
            store_h(1, s, dot3(ah, al, abuf[s * 2], abuf[s * 2 + 1]), 4, UR, t * 64)

        loop(0, 4, quarter)

    def second(group, v):
        cols = pl.ds(group * 256, 256)
        r = None
        for s in range(2):
            t = dot3(abuf[4 + s * 2, :, cols], abuf[5 + s * 2, :, cols], hbuf[group, s, 0, v], hbuf[group, s, 1, v])
            r = t if r is None else r + t
        if group == 1:
            z[v] = r
        else:
            z[v] += r

    relay(0)
    relay(1)
    mix_low(0, send=False)
    relay(2)
    mix_low(1, send=False)
    loop(1, nsector, lambda d: share(d).wait_recv())
    for n in range(4):
        for i in range(4):
            own[SHARED[n], :, pl.ds(i % 2 * UR, UR), pl.ds(i // 2 * 256, 256)] = got[
                chosen[n % 2 * 4 + i], :, :, pl.ds(n // 2 * 256, 256)]
    issue(3)
    issue(4)
    issue(5)
    f1(0).start()
    f1(1).start()
    shift().start()
    mix_low(2)
    relay(3)
    issue(6)
    relay(4)
    mix_shared(0)
    issue(7)
    relay(5)
    mix_shared(1)
    issue(8)
    give_back(0)
    relay(6)
    mix_shared(2)
    issue(9)
    relay(7)
    mix_shared(3)
    give_back(1)
    shift().wait_recv()
    issue(10)
    relay(8)
    mix_low(3)
    issue(11)
    relay(9)
    assemble(0, A0, size_here)
    issue(12)
    relay(10)
    mix_low(4)
    issue(13)
    first_low(0, 0)
    relay(11)
    assemble(1, A1, size_prev)
    issue(14)
    relay(12)
    mix_low(5)
    relay(13)
    mix_low(6)
    relay(14)
    mix_low(7)
    first_low(0, 1)
    given(0)
    first_shared(0)
    arrived(PSI)
    for d in range(4):
        row0 = pl.multiple_of(((y + d) % 4) * 128, 128)
        for h, part in enumerate(halves(piece(d, PSI).reshape(128, 512))):
            pbuf[h, pl.ds(row0, 128), :] = part

    loop(0, 4, lambda e: f1(e).wait_recv())
    first_low(1, 0)
    given(1)
    first_shared(1)
    loop(0, 4, lambda v: second(1, v))
    loop(4, 8, lambda e: f1(e).wait_recv())
    first_low(1, 1)

    def exchange(v):
        return remote(z.at[v], zp.at[v], zp_send.at[v], zp_recv.at[v], other)

    def out(v):
        return pltpu.make_async_copy(z.at[v], fresh.at[v], out_sem.at[v])

    def finish(v):
        second(0, v)
        exchange(v).start()
        out(v).start()

    loop(0, 4, finish)

    def apply_left(v):
        exchange(v).wait_recv()
        lh, ll = halves(jnp.where(section == 0, z[v], zp[v]))
        x = dot3(lh, ll, pbuf[0], pbuf[1]) * center[0, y * 4 + v]
        return halves(x), halves(jnp.where(section == 0, zp[v], z[v]))

    total[...] = jnp.zeros_like(total)

    def add(v):
        (xh, xl), (rh, rl) = apply_left(v)
        total[...] += dot3(xh, xl, rh, rl)

    loop(0, 3, add)
    for h, (x, r) in enumerate(zip(*apply_left(3))):
        hbuf[0, 0, h, 0] = x[:256]
        hbuf[0, 1, h, 0] = x[256:]
        abuf[h] = r

    def partial(slot, b):
        rows = pl.ds(pl.multiple_of((b % 2) * 128, 128), 128)
        r = dot3(hbuf[0, b // 2, 0, 0, rows, :], hbuf[0, b // 2, 1, 0, rows, :], abuf[0], abuf[1])
        r += total[pl.ds(pl.multiple_of(b * 128, 128), 128), :]
        q[slot, 0] = r[:, :256]
        q[slot, 1] = r[:, 256:]

    hops = [
        remote(src, dst, rs_send.at[i], rs_recv.at[i], to) for i, (src, dst, to) in enumerate((
            (q.at[0, 0], s1.at[0], right),
            (q.at[0, 1], s1.at[1], left),
            (q.at[1, 1], s2.at[0, 1], right),
            (q.at[2, 0], s2.at[1, 0], left),
            (q.at[1, 0], s2.at[0, 0], right),
            (q.at[2, 1], s2.at[1, 1], left),
        ))
    ]

    partial(0, (y + 2) % 4)
    hops[0].start()
    hops[1].start()
    partial(1, (y + 1) % 4)
    hops[2].start()
    partial(2, (y + 3) % 4)
    hops[3].start()
    hops[0].wait_recv()
    q[1, 0] += s1[0]
    hops[4].start()
    hops[1].wait_recv()
    q[2, 1] += s1[1]
    hops[5].start()
    partial(3, y)
    for i in range(2, 6):
        hops[i].wait_recv()
    for t in range(2):
        hpsi[:, pl.ds(t * 256, 256)] = q[3, t] + (s2[0, t] + s2[1, t])

    for hop in hops:
        hop.wait_send()
    shift().wait_send()
    for k in range(NK):
        to_right(k).wait_send()
        to_left(k).wait_send()
        on_right(k).wait_send()
        on_left(k).wait_send()
    loop(0, NL, lambda e: f1(e).wait_send())
    for h in range(2):
        for s in range(2):
            give(h, s, 1 - s).wait_send()
            loop(2, nsector, lambda d, h=h, s=s: give(h, s, d).wait_send())

    def last(v):
        exchange(v).wait_send()
        out(v).wait()

    loop(0, 4, last)


def settle(src, dst, held, came, gone):
    def part(ref, i):
        return ref.at[i // 4, pl.ds(i % 4 * 128, 128), :]

    incoming = [pltpu.make_async_copy(part(src, i), held.at[i], came.at[i]) for i in range(16)]
    outgoing = [pltpu.make_async_copy(held.at[i], part(dst, i), gone.at[i]) for i in range(16)]
    for copy in incoming:
        copy.start()
    for i in range(16):
        incoming[i].wait()
        outgoing[i].start()
    for copy in outgoing:
        copy.wait()


def local(env, site, sector_tiles, mpo_mask, mpo_coef, psi, center_coef):
    anywhere = pl.BlockSpec(memory_space=pl.ANY)
    scalars = pl.BlockSpec(memory_space=pltpu.SMEM)
    dma = pltpu.SemaphoreType.DMA
    fresh, hpsi = pl.pallas_call(
        functools.partial(kernel, sector_tiles.shape[0]),
        out_shape=(
            jax.ShapeDtypeStruct((4, 512, 512), F32),
            jax.ShapeDtypeStruct((128, 512), F32),
        ),
        in_specs=[anywhere, pl.BlockSpec(memory_space=pltpu.VMEM), anywhere, scalars, scalars, scalars, scalars],
        out_specs=(anywhere, pl.BlockSpec(memory_space=pltpu.VMEM)),
        scratch_shapes=[
            pltpu.VMEM((NK, 4, CH, 512), F32),
            pltpu.VMEM((3, NK, 4, CH, 512), F32),
            pltpu.VMEM((NL, 4, CH, 512), F32),
            pltpu.VMEM((NL, 4, CH, 512), F32),
            pltpu.VMEM((NL, 4, CH, 512), F32),
            pltpu.VMEM((16, 4, UR, 512), F32),
            pltpu.VMEM((16, 4, UR, 512), F32),
            pltpu.VMEM((16, 4, UR, 512), F32),
            pltpu.VMEM((2, 2, 8, 4, UR, 256), F32),
            pltpu.VMEM((16, 4, UR, 512), F32),
            pltpu.VMEM((16, 4, UR, 512), F32),
            pltpu.VMEM((2, 2, 2, 4, 256, 512), BF16),
            pltpu.VMEM((4, 512, 512), F32),
            pltpu.VMEM((4, 512, 512), F32),
            pltpu.VMEM((8, 512, 512), BF16),
            pltpu.VMEM((2, 512, 512), BF16),
            pltpu.VMEM((4, CH, 512), F32),
            pltpu.VMEM((512, 512), F32),
            pltpu.VMEM((4, 2, 128, 256), F32),
            pltpu.VMEM((2, 128, 256), F32),
            pltpu.VMEM((2, 2, 128, 256), F32),
            pltpu.SMEM((128,), F32),
            pltpu.SMEM((48,), jnp.int32),
            dma((NK,)), dma((16,)), dma((2,)), dma((2, NK)), dma((2, NK)), dma((2, NK)), dma((2, NK)),
            dma((NL,)), dma((NL,)), dma((16,)), dma((16,)), dma((2, 2, 16)), dma((2, 2, 16)),
            dma((4,)), dma((4,)), dma((4,)), dma((6,)), dma((6,)),
        ],
        compiler_params=pltpu.CompilerParams(
            collective_id=0, has_side_effects=True, vmem_limit_bytes=62 << 20
        ),
        name="window",
    )(env[0], site[0], psi[0].reshape(4, CH, 512), sector_tiles, mpo_mask, mpo_coef, center_coef)
    fresh = pl.pallas_call(
        settle,
        out_shape=jax.ShapeDtypeStruct((4, 512, 512), F32),
        in_specs=[anywhere],
        out_specs=anywhere,
        scratch_shapes=[pltpu.VMEM((16, 128, 512), F32), dma((16,)), dma((16,))],
        name="settle",
    )(fresh)
    return fresh[None], hpsi[None]


def solution(mesh):
    placed = (
        P("section", "block", None, None),
        P("section", "block", None, None),
        P(),
        P("section", None, None),
        P("section", None, None, None),
        P("section", "block", None),
        P("section", None),
    )
    return jax.shard_map(
        local,
        mesh=mesh,
        in_specs=placed,
        out_specs=(P("section", "block", None, None), P("section", "block", None)),
        check_vma=False,
    )
```

```python
import functools

import jax
import jax.numpy as jnp
from jax import lax
from jax.experimental import pallas as pl
from jax.experimental.pallas import tpu as pltpu
from jax.sharding import PartitionSpec as P

TROW = 32
CH = 32
UR = 16
NL = 8
LOW = (0, 1, 2, 7, 9, 11, 12, 13)
A0, A1, PSI = 8, 10, 14
SHARED = (3, 4, 5, 6)
NK = 15
ORDER = (1, 4, 15, 12, 5, 11, 3, 13, 2, 8, 6, 9, 14, 7, 10)
MESH = pl.DeviceIdType.MESH
F32, BF16 = jnp.float32, jnp.bfloat16


def halves(value):
    high = value.astype(BF16)
    low = (value - high.astype(F32)).astype(BF16)
    return high, low


def dot3(ah, al, bh, bl):
    dot = functools.partial(jnp.dot, preferred_element_type=F32)
    return dot(ah, bh) + (dot(ah, bl) + dot(al, bh))


def kernel(nsector, env, site, psi, tiles, mask, coef, center, fresh, hpsi,
           own, rcv, f0, f1s, f1r, up, pack, got, fu, back0, back1, hbuf, z, zp, abuf, pbuf, stage, total, q, s1, s2, table, place,
           load_sem, up_sem, shift_sem, own_send, own_recv, fwd_send, fwd_recv, f1_send, f1_recv,
           sh_send, sh_recv, bk_send, bk_recv, zp_send, zp_recv, out_sem, rs_send, rs_recv):
    section = lax.axis_index("section")
    block = lax.axis_index("block")
    sector = block // 4
    y = block % 4
    base = block - y
    right = (section, base + (y + 1) % 4)
    left = (section, base + (y + 3) % 4)
    other = (1 - section, block)

    def ring(distance):
        return (section, ((sector + distance + nsector) % nsector) * 4 + y)

    above = ring(1)

    def remote(src, dst, send, recv, to):
        return pltpu.make_async_remote_copy(
            src_ref=src, dst_ref=dst, send_sem=send, recv_sem=recv, device_id=to, device_id_type=MESH)

    def loop(lo, hi, body):
        lax.fori_loop(lo, hi, lambda i, c: (body(i), c)[1], 0)

    def load(k):
        if k == PSI:
            src = psi
        else:
            src = env.at[:, pl.ds(LOW.index(k) * CH, CH), :]
        return pltpu.make_async_copy(src, own.at[k], load_sem.at[k])

    def load_up(u):
        rows = pl.ds(pl.multiple_of(256 + u * UR, UR), UR)
        return pltpu.make_async_copy(env.at[:, rows, :], up.at[u], up_sem.at[u])

    load(0).start()
    loop(0, nsector, lambda u: load_up(u).start())
    for k in LOW[1:] + (PSI,):
        load(k).start()

    barrier = pltpu.get_barrier_semaphore()
    for peer in (right, left, other):
        pl.semaphore_signal(barrier, inc=1, device_id=peer, device_id_type=MESH)
    loop(1, nsector, lambda d: pl.semaphore_signal(barrier, inc=1, device_id=ring(d), device_id_type=MESH))
    pl.semaphore_wait(barrier, nsector + 2)

    def shift():
        return remote(stage, own.at[A1], shift_sem.at[0], shift_sem.at[1], above)

    def rows_of(k):
        return pl.ds(0, CH)

    def to_right(k):
        r = rows_of(k)
        return remote(own.at[k, :, r], rcv.at[2, k, :, r], own_send.at[0, k], own_recv.at[0, k], right)

    def to_left(k):
        r = rows_of(k)
        return remote(own.at[k, :, r], rcv.at[0, k, :, r], own_send.at[1, k], own_recv.at[1, k], left)

    def on_right(k):
        r = rows_of(k)
        return remote(rcv.at[2, k, pl.ds(0, 2), r], rcv.at[1, k, pl.ds(0, 2), r],
                      fwd_send.at[0, k], fwd_recv.at[0, k], right)

    def on_left(k):
        r = rows_of(k)
        return remote(rcv.at[0, k, pl.ds(2, 2), r], rcv.at[1, k, pl.ds(2, 2), r],
                      fwd_send.at[1, k], fwd_recv.at[1, k], left)

    def issue(k):
        if k in LOW + (PSI,):
            load(k).wait()
        to_right(k).start()
        to_left(k).start()

    def relay(k):
        to_right(k).wait_recv()
        on_right(k).start()
        to_left(k).wait_recv()
        on_left(k).start()

    def arrived(k):
        on_right(k).wait_recv()
        on_left(k).wait_recv()

    issue(0)

    start = 0
    for i in range(nsector):
        count = jnp.maximum(2 * (tiles[i] - 8), 0)
        place[i] = start % 16
        place[16 + i] = count
        start = start + count

    def share(d):
        return remote(pack.at[d], got.at[d], sh_send.at[d], sh_recv.at[d], ring(d))

    loop(0, nsector, lambda u: load_up(u).wait())

    def unit_for(d):
        return (sector + d + 16 - place[sector]) % 16

    got[0] = up[unit_for(0)]

    def send_share(d):
        pack[d] = up[unit_for(d)]
        share(d).start()

    for d in ORDER:
        send_share(d)
    issue(1)
    issue(2)
    own[A0] = site[:, 0, :].reshape(4, CH, 512)
    stage[...] = site[:, 1, :].reshape(4, CH, 512)

    for s in range(2):
        for d in range(4):
            for j in range(4):
                w = ((y + d) % 4) * 4 + j
                for v in range(4):
                    c = coef[0, s, w, y * 4 + v] * mask[0, w, y * 4 + v].astype(F32)
                    table[(s * 4 + v) * 16 + d * 4 + j] = c

    rank = 0
    chosen = [0] * 8
    for d in range(nsector):
        home = (sector - d + 16) % 16
        valid = (sector + 16 - place[home]) % 16 < place[16 + home]
        place[32 + d] = jnp.where(valid, rank, 0)
        for j in range(7):
            chosen[j] = jnp.where(valid & (rank == j), d, chosen[j])
        rank = rank + valid.astype(jnp.int32)

    size_here = tiles[sector] * TROW
    before = (sector + nsector - 1) % nsector
    size_prev = jnp.where(sector > 0, tiles[before] * TROW, 0)

    def piece(d, k):
        return own[k] if d == 0 else rcv[d - 1, k]

    def assemble(s, k, rows_kept):
        arrived(k)
        for d in range(4):
            row0 = pl.multiple_of(((y + d) % 4) * 128, 128)
            v = piece(d, k).reshape(128, 512)
            i = lax.broadcasted_iota(jnp.int32, (128, 512), 0) + row0
            j = lax.broadcasted_iota(jnp.int32, (128, 512), 1)
            v = jnp.where((i < rows_kept) & (j < size_here), v, 0.0)
            t = v.T
            for h, (a, b) in enumerate(zip(halves(v), halves(t))):
                abuf[s * 2 + h, pl.ds(row0, 128), :] = a
                abuf[4 + s * 2 + h, :, pl.ds(row0, 128)] = b

    def f1(e):
        return remote(f1s.at[e], f1r.at[e], f1_send.at[e], f1_recv.at[e], above)

    def mix(k, nrows, put):
        arrived(k)

        def rows(r):
            span = pl.ds(pl.multiple_of(r * 8, 8), 8)
            acc = [None] * 8
            for d in range(4):
                for j in range(4):
                    x = own[k, j, span, :] if d == 0 else rcv[d - 1, k, j, span, :]
                    for o in range(8):
                        term = table[o * 16 + d * 4 + j] * x
                        acc[o] = term if acc[o] is None else acc[o] + term
            put(r, acc)

        loop(0, nrows // 8, rows)

    def mix_low(e, send=True):
        def put(r, acc):
            span = pl.ds(pl.multiple_of(r * 8, 8), 8)
            for v in range(4):
                f0[e, v, span, :] = acc[v]
                f1s[e, v, span, :] = acc[4 + v]

        mix(LOW[e], CH, put)
        if send:
            f1(e).start()

    def mix_shared(n):
        def put(r, acc):
            span = pl.ds(pl.multiple_of((r % 2) * 8, 8), 8)
            for o in range(8):
                for c in range(2):
                    unit = n % 2 * 4 + 2 * c + r // 2
                    fu[n // 2, o // 4, unit, o % 4, span, :] = acc[o][:, c * 256:c * 256 + 256]

        mix(SHARED[n], CH, put)

    back = (back0, back1)

    def give(h, s, d):
        source = pack if s == 0 else up
        to = ring(nsector - d + s)
        cols = pl.ds(h * 256, 256)
        return remote(source.at[d, :, :, cols], back[s].at[d, :, :, cols], bk_send.at[h, s, d], bk_recv.at[h, s, d], to)

    def give_back(h):
        cols = pl.ds(h * 256, 256)
        if h == 0:
            loop(1, nsector, lambda d: share(d).wait_send())
        back0[0, :, :, cols] = fu[h, 0, place[32]]
        back1[1, :, :, cols] = fu[h, 1, place[33]]

        def send(s, d):
            (pack if s == 0 else up)[d, :, :, cols] = fu[h, s, place[32 + d]]
            give(h, s, d).start()

        for d in ORDER:
            send(0, 16 - d)
        for d in ORDER:
            send(1, (17 - d) % 16)

    def given(s):
        for h in range(2):
            give(h, s, 1 - s).wait_recv()
            loop(2, nsector, lambda d, h=h: give(h, s, d).wait_recv())

    def store_h(group, s, r, count, rows, at):
        for h, part in enumerate(halves(r)):
            part = part.reshape(count, 4, rows, 512)
            for u in range(count):
                for v in range(4):
                    hbuf[group, s, h, v, pl.ds(pl.multiple_of(at + u * rows, 16), rows), :] = part[u, v]

    def first_low(s, g, lo=0, hi=2):
        def half(t):
            at = 4 * g + 2 * t
            lhs = (f0 if s == 0 else f1r)[pl.ds(at, 2)]
            ah, al = halves(lhs.reshape(256, 512))
            store_h(0, s, dot3(ah, al, abuf[s * 2], abuf[s * 2 + 1]), 2, CH, at * CH)

        loop(lo, hi, half)

    def first_shared(s):
        home = sector if s == 0 else before

        def quarter(t):
            units = [back[s][(4 * t + i + place[home] + 16 - home) % 16] for i in range(4)]
            ah, al = halves(jnp.concatenate([u.reshape(64, 512) for u in units], axis=0))
            store_h(1, s, dot3(ah, al, abuf[s * 2], abuf[s * 2 + 1]), 4, UR, t * 64)

        loop(0, 4, quarter)

    def second(group, v, spins=(0, 1)):
        cols = pl.ds(group * 256, 256)
        r = None
        for s in spins:
            t = dot3(abuf[4 + s * 2, :, cols], abuf[5 + s * 2, :, cols], hbuf[group, s, 0, v], hbuf[group, s, 1, v])
            r = t if r is None else r + t
        if group == 1:
            z[v] = r
        else:
            z[v] += r

    relay(0)
    relay(1)
    mix_low(0, send=False)
    relay(2)
    mix_low(1, send=False)
    loop(1, nsector, lambda d: share(d).wait_recv())
    for n in range(4):
        for i in range(4):
            own[SHARED[n], :, pl.ds(i % 2 * UR, UR), pl.ds(i // 2 * 256, 256)] = got[
                chosen[n % 2 * 4 + i], :, :, pl.ds(n // 2 * 256, 256)]
    issue(3)
    issue(4)
    issue(5)
    f1(0).start()
    f1(1).start()
    shift().start()
    mix_low(2)
    relay(3)
    issue(6)
    relay(4)
    mix_shared(0)
    issue(7)
    relay(5)
    mix_shared(1)
    issue(8)
    give_back(0)
    relay(6)
    mix_shared(2)
    issue(9)
    relay(7)
    mix_shared(3)
    give_back(1)
    shift().wait_recv()
    issue(10)
    relay(8)
    mix_low(3)
    issue(11)
    relay(9)
    assemble(0, A0, size_here)
    issue(12)
    relay(10)
    mix_low(4)
    issue(13)
    first_low(0, 0)
    relay(11)
    assemble(1, A1, size_prev)
    issue(14)
    relay(12)
    mix_low(5)
    relay(13)
    mix_low(6)
    relay(14)
    mix_low(7)
    first_low(0, 1)
    given(0)
    first_shared(0)
    arrived(PSI)
    for d in range(4):
        row0 = pl.multiple_of(((y + d) % 4) * 128, 128)
        for h, part in enumerate(halves(piece(d, PSI).reshape(128, 512))):
            pbuf[h, pl.ds(row0, 128), :] = part

    loop(0, 4, lambda e: f1(e).wait_recv())
    first_low(1, 0)
    given(1)
    first_shared(1)
    loop(0, 4, lambda v: second(1, v))
    loop(0, 4, lambda v: second(0, v, (0,)))
    for t in range(2):
        loop(4 + 2 * t, 6 + 2 * t, lambda e: f1(e).wait_recv())
        first_low(1, 1, t, t + 1)

    def exchange(v):
        return remote(z.at[v], zp.at[v], zp_send.at[v], zp_recv.at[v], other)

    def out(v):
        return pltpu.make_async_copy(z.at[v], fresh.at[v], out_sem.at[v])

    def finish(v):
        second(0, v, (1,))
        exchange(v).start()
        out(v).start()

    loop(0, 4, finish)

    def apply_left(v):
        exchange(v).wait_recv()
        lh, ll = halves(jnp.where(section == 0, z[v], zp[v]))
        x = dot3(lh, ll, pbuf[0], pbuf[1]) * center[0, y * 4 + v]
        return halves(x), halves(jnp.where(section == 0, zp[v], z[v]))

    total[...] = jnp.zeros_like(total)

    def add(v):
        (xh, xl), (rh, rl) = apply_left(v)
        total[...] += dot3(xh, xl, rh, rl)

    loop(0, 3, add)
    for h, (x, r) in enumerate(zip(*apply_left(3))):
        hbuf[0, 0, h, 0] = x[:256]
        hbuf[0, 1, h, 0] = x[256:]
        abuf[h] = r

    def partial(slot, b):
        rows = pl.ds(pl.multiple_of((b % 2) * 128, 128), 128)
        r = dot3(hbuf[0, b // 2, 0, 0, rows, :], hbuf[0, b // 2, 1, 0, rows, :], abuf[0], abuf[1])
        r += total[pl.ds(pl.multiple_of(b * 128, 128), 128), :]
        q[slot, 0] = r[:, :256]
        q[slot, 1] = r[:, 256:]

    hops = [
        remote(src, dst, rs_send.at[i], rs_recv.at[i], to) for i, (src, dst, to) in enumerate((
            (q.at[0, 0], s1.at[0], right),
            (q.at[0, 1], s1.at[1], left),
            (q.at[1, 1], s2.at[0, 1], right),
            (q.at[2, 0], s2.at[1, 0], left),
            (q.at[1, 0], s2.at[0, 0], right),
            (q.at[2, 1], s2.at[1, 1], left),
        ))
    ]

    partial(0, (y + 2) % 4)
    hops[0].start()
    hops[1].start()
    partial(1, (y + 1) % 4)
    hops[2].start()
    partial(2, (y + 3) % 4)
    hops[3].start()
    hops[0].wait_recv()
    q[1, 0] += s1[0]
    hops[4].start()
    hops[1].wait_recv()
    q[2, 1] += s1[1]
    hops[5].start()
    partial(3, y)
    for i in range(2, 6):
        hops[i].wait_recv()
    for t in range(2):
        hpsi[:, pl.ds(t * 256, 256)] = q[3, t] + (s2[0, t] + s2[1, t])

    for hop in hops:
        hop.wait_send()
    shift().wait_send()
    for k in range(NK):
        to_right(k).wait_send()
        to_left(k).wait_send()
        on_right(k).wait_send()
        on_left(k).wait_send()
    loop(0, NL, lambda e: f1(e).wait_send())
    for h in range(2):
        for s in range(2):
            give(h, s, 1 - s).wait_send()
            loop(2, nsector, lambda d, h=h, s=s: give(h, s, d).wait_send())

    def last(v):
        exchange(v).wait_send()
        out(v).wait()

    loop(0, 4, last)


def settle(src, dst, held, came, gone):
    def part(ref, i):
        return ref.at[i // 4, pl.ds(i % 4 * 128, 128), :]

    incoming = [pltpu.make_async_copy(part(src, i), held.at[i], came.at[i]) for i in range(16)]
    outgoing = [pltpu.make_async_copy(held.at[i], part(dst, i), gone.at[i]) for i in range(16)]
    for copy in incoming:
        copy.start()
    for i in range(16):
        incoming[i].wait()
        outgoing[i].start()
    for copy in outgoing:
        copy.wait()


def local(env, site, sector_tiles, mpo_mask, mpo_coef, psi, center_coef):
    anywhere = pl.BlockSpec(memory_space=pl.ANY)
    scalars = pl.BlockSpec(memory_space=pltpu.SMEM)
    dma = pltpu.SemaphoreType.DMA
    fresh, hpsi = pl.pallas_call(
        functools.partial(kernel, sector_tiles.shape[0]),
        out_shape=(
            jax.ShapeDtypeStruct((4, 512, 512), F32),
            jax.ShapeDtypeStruct((128, 512), F32),
        ),
        in_specs=[anywhere, pl.BlockSpec(memory_space=pltpu.VMEM), anywhere, scalars, scalars, scalars, scalars],
        out_specs=(anywhere, pl.BlockSpec(memory_space=pltpu.VMEM)),
        scratch_shapes=[
            pltpu.VMEM((NK, 4, CH, 512), F32),
            pltpu.VMEM((3, NK, 4, CH, 512), F32),
            pltpu.VMEM((NL, 4, CH, 512), F32),
            pltpu.VMEM((NL, 4, CH, 512), F32),
            pltpu.VMEM((NL, 4, CH, 512), F32),
            pltpu.VMEM((16, 4, UR, 512), F32),
            pltpu.VMEM((16, 4, UR, 512), F32),
            pltpu.VMEM((16, 4, UR, 512), F32),
            pltpu.VMEM((2, 2, 8, 4, UR, 256), F32),
            pltpu.VMEM((16, 4, UR, 512), F32),
            pltpu.VMEM((16, 4, UR, 512), F32),
            pltpu.VMEM((2, 2, 2, 4, 256, 512), BF16),
            pltpu.VMEM((4, 512, 512), F32),
            pltpu.VMEM((4, 512, 512), F32),
            pltpu.VMEM((8, 512, 512), BF16),
            pltpu.VMEM((2, 512, 512), BF16),
            pltpu.VMEM((4, CH, 512), F32),
            pltpu.VMEM((512, 512), F32),
            pltpu.VMEM((4, 2, 128, 256), F32),
            pltpu.VMEM((2, 128, 256), F32),
            pltpu.VMEM((2, 2, 128, 256), F32),
            pltpu.SMEM((128,), F32),
            pltpu.SMEM((48,), jnp.int32),
            dma((NK,)), dma((16,)), dma((2,)), dma((2, NK)), dma((2, NK)), dma((2, NK)), dma((2, NK)),
            dma((NL,)), dma((NL,)), dma((16,)), dma((16,)), dma((2, 2, 16)), dma((2, 2, 16)),
            dma((4,)), dma((4,)), dma((4,)), dma((6,)), dma((6,)),
        ],
        compiler_params=pltpu.CompilerParams(
            collective_id=0, has_side_effects=True, vmem_limit_bytes=62 << 20
        ),
        name="window",
    )(env[0], site[0], psi[0].reshape(4, CH, 512), sector_tiles, mpo_mask, mpo_coef, center_coef)
    fresh = pl.pallas_call(
        settle,
        out_shape=jax.ShapeDtypeStruct((4, 512, 512), F32),
        in_specs=[anywhere],
        out_specs=anywhere,
        scratch_shapes=[pltpu.VMEM((16, 128, 512), F32), dma((16,)), dma((16,))],
        name="settle",
    )(fresh)
    return fresh[None], hpsi[None]


def solution(mesh):
    placed = (
        P("section", "block", None, None),
        P("section", "block", None, None),
        P(),
        P("section", None, None),
        P("section", None, None, None),
        P("section", "block", None),
        P("section", None),
    )
    return jax.shard_map(
        local,
        mesh=mesh,
        in_specs=placed,
        out_specs=(P("section", "block", None, None), P("section", "block", None)),
        check_vma=False,
    )
```
